32 devices in a mesh: seq: 8 (over y, x, core), head: 4 (over z).
Axes of the slice: x: 2, y: 2, z: 4, core: 2. Of those that a mesh axis runs over, the one named last changes fastest.
Arguments:
- stream: bfloat16 [8192, 1536], P('seq'), may hold values from -6 to 6
- prescale: float32 [1536], replicated, may hold values from 0.25 to 1.75
- gelumat: bfloat16 [1536, 2048], P(None, 'head'), may hold values from -0.15625 to 0.15625
- gelubias: float32 [2048], P('head'), may hold values from -3 to 3
- lrumat: bfloat16 [1536, 2048], P(None, 'head'), may hold values from -0.15625 to 0.15625
- lrubias: float32 [2048], P('head'), may hold values from -3 to 3
- convtaps: float32 [4, 2048], P(None, 'head'), may hold values from -3 to 3
- convbias: float32 [2048], P('head'), may hold values from -2 to 2
- recgates: bfloat16 [16, 128, 128], P('head'), may hold values from -0.5 to 0.5
- recbias: float32 [2048], P('head'), may hold values from -3 to 3
- inpgates: bfloat16 [16, 128, 128], P('head'), may hold values from -0.5 to 0.5
- inpbias: float32 [2048], P('head'), may hold values from -3 to 3
- lambdas: float32 [2048], P('head'), may hold values from 4 to 16
- outmat: bfloat16 [2048, 1536], P('head'), may hold values from -0.375 to 0.375
- midscale: float32 [1536], replicated, may hold values from 0.25 to 1.75
- gatemat: bfloat16 [1536, 4608], P(None, 'head'), may hold values from -0.15625 to 0.15625
- upmatrix: bfloat16 [1536, 4608], P(None, 'head'), may hold values from -0.15625 to 0.15625
- downmat: bfloat16 [4608, 1536], P('head'), may hold values from -0.1875 to 0.1875
- resets: int32 [8192], P('seq'), may hold values from 0 to 1, as said below
- cotangent: bfloat16 [8192, 1536], P('seq'), may hold values from -6 to 6
Outputs:
- block_output: bfloat16 [8192, 1536], P('seq')
- grad_stream: bfloat16 [8192, 1536], P('seq')
- grad_prescale: float32 [1536], P('seq')
- grad_gelumat: float32 [1536, 2048], P('seq', 'head')
- grad_gelubias: float32 [2048], P('head')
- grad_lrumat: float32 [1536, 2048], P('seq', 'head')
- grad_lrubias: float32 [2048], P('head')
- grad_convtaps: float32 [4, 2048], P(None, 'head')
- grad_convbias: float32 [2048], P('head')
- grad_recgates: float32 [16, 128, 128], P('head')
- grad_recbias: float32 [2048], P('head')
- grad_inpgates: float32 [16, 128, 128], P('head')
- grad_inpbias: float32 [2048], P('head')
- grad_lambdas: float32 [2048], P('head')
- grad_outmat: float32 [2048, 1536], P('head', 'seq')
- grad_midscale: float32 [1536], P('seq')
- grad_gatemat: float32 [1536, 4608], P('seq', 'head')
- grad_upmatrix: float32 [1536, 4608], P('seq', 'head')
- grad_downmat: float32 [4608, 1536], P('head', 'seq')
The draws below stay inside these ranges and needn't reach their ends.
Inputs may be any that keep to these rules, and one draw needn't show every extreme that they name: `resets`: position 0 is a document start. One document starts within the first 512 tokens and ends within the last 512 tokens of the stream.
All inputs are finite; a program needn't handle non-finite values.
Results may differ from the reference program's by a relative error of at most 0.025.
Values may be sent and summed in bfloat16 or wider, within the bound.
No kernel may reach another device: no remote copies, remote signals or barrier semaphores. Data moves between devices by JAX's collectives and lax.ppermute only.
A program may use at most 192 MiB of HBM per device.

```python
import math
import jax
import jax.numpy as jnp
from jax import lax

D = 1536
R = 2048
FF = 4608
KCONV = 4
BLK = 128
TOK_DEV = 1024
TOKENS = 8192


def draw_lambdas(key, part):
    key = jax.random.fold_in(key, 11)
    fraction = jax.random.uniform(key, (R,), jnp.float32)
    low_end = math.log(0.25 / TOKENS)
    high_end = math.log(1.0 / 160.0)
    rate = jnp.exp(low_end + (high_end - low_end) * fraction)
    return -jnp.log(jnp.expm1(rate))


def draw_resets(key, part):
    key = jax.random.fold_in(key, 5)
    first, second, third = jax.random.split(key, 3)
    start = jax.random.randint(first, (), 1, TOK_DEV // 2)
    finish = jax.random.randint(second, (), TOKENS - TOK_DEV // 2, TOKENS)
    places = jnp.arange(TOKENS, dtype=jnp.int32)
    coins = jax.random.randint(third, (TOKENS,), 0, 24)
    outside = (places < start) | (places > finish)
    flags = (coins == 0) & outside | (places == 0) | (places == start) | (places == finish)
    return jnp.where(flags, 1, 0).astype(jnp.int32)


def level_of(key, extent, pieces, least, top_value):
    def one(position, shards_of):
        steps = jax.random.uniform(jax.random.fold_in(jax.random.fold_in(key, 6), position), (shards_of,), jnp.float32, least / len(pieces), top_value / len(pieces))
        return jnp.repeat(jnp.exp(steps), extent[position] // shards_of).reshape((-1,) + (1,) * (len(extent) - position - 1))

    level = one(*pieces[0])
    for cut in pieces[1:]:
        level = level * one(*cut)
    return level


def centred(rng, dims, spread, bound, shards=(), kind=jnp.bfloat16):
    array = spread * jax.random.normal(rng, dims, jnp.float32)
    if shards:
        array = array * level_of(rng, dims, shards, -0.22, 0.18)
    return jnp.clip(array, -bound, bound).astype(kind)


def setup_inputs(seed: int = 0) -> dict:
    key_of = jax.random.split(jax.random.key(seed), 21)
    return {
        "stream": centred(key_of[0], (TOKENS, D), 1.0, 6.0, ((0, 8),)),
        "prescale": jnp.clip(1.0 + 0.15 * jax.random.normal(key_of[1], (D,), jnp.float32), 0.25, 1.75),
        "gelumat": centred(key_of[2], (D, R), D ** -0.5, 0.15625, ((1, 4),)),
        "gelubias": centred(key_of[3], (R,), 0.5, 3.0, ((0, 4),), jnp.float32),
        "lrumat": centred(key_of[4], (D, R), D ** -0.5, 0.15625, ((1, 4),)),
        "lrubias": centred(key_of[5], (R,), 0.5, 3.0, ((0, 4),), jnp.float32),
        "convtaps": centred(key_of[6], (KCONV, R), KCONV ** -0.5, 3.0, ((1, 4),), jnp.float32),
        "convbias": centred(key_of[7], (R,), 0.3, 2.0, ((0, 4),), jnp.float32),
        "recgates": centred(key_of[8], (R // BLK, BLK, BLK), BLK ** -0.5, 0.5, ((0, 4),)),
        "recbias": centred(key_of[9], (R,), 0.5, 3.0, ((0, 4),), jnp.float32),
        "inpgates": centred(key_of[10], (R // BLK, BLK, BLK), BLK ** -0.5, 0.5, ((0, 4),)),
        "inpbias": centred(key_of[11], (R,), 0.5, 3.0, ((0, 4),), jnp.float32),
        "lambdas": draw_lambdas(jax.random.fold_in(key_of[20], 71), 0),
        "outmat": centred(key_of[13], (R, D), (R // 8) ** -0.5, 0.375, ((0, 4),)),
        "midscale": jnp.clip(1.0 + 0.15 * jax.random.normal(key_of[14], (D,), jnp.float32), 0.25, 1.75),
        "gatemat": centred(key_of[15], (D, FF), D ** -0.5, 0.15625, ((1, 4),)),
        "upmatrix": centred(key_of[16], (D, FF), D ** -0.5, 0.15625, ((1, 4),)),
        "downmat": centred(key_of[17], (FF, D), (FF // 4) ** -0.5, 0.1875, ((0, 4),)),
        "resets": draw_resets(jax.random.fold_in(key_of[20], 71), 0),
        "cotangent": centred(key_of[19], (TOKENS, D), 1.0, 6.0, ((0, 8),)),
    }


@jax.custom_vjp
def low(v):
    return lax.optimization_barrier(v.astype(jnp.bfloat16)).astype(jnp.float32)

@jax.custom_vjp
def low_back(v):
    return v

def low_keep(v):
    return (low(v), None)

def low_pass(kept, grad):
    return (grad,)

def back_keep(v):
    return (v, None)

def back_low(kept, grad):
    return (low(grad),)
low.defvjp(low_keep, low_pass)
low_back.defvjp(back_keep, back_low)
eps = 1e-06
lru_power = 8.0
high = lax.Precision.HIGHEST

def rms_scale(v, gain):
    return v * lax.rsqrt(lax.optimization_barrier(jnp.mean(v * v, axis=-1, keepdims=True)) + eps) * gain

def link(earlier, later):
    return (earlier[0] * later[0], later[0] * earlier[1] + later[1])

def gelu_tanh(v):
    return jax.nn.gelu(v, approximate=True)

def forward(x, g1, wy, by, wx, bx, conv_w, conv_b, wa, ba, wi, bi, lam, wo, g2, wg, wu, wd, flags):
    n1 = low(rms_scale(x, g1))
    ypre = low_back(jnp.dot(n1, wy, precision=high) + by)
    y = gelu_tanh(ypre)
    u = low_back(low(jnp.dot(n1, wx, precision=high) + bx))
    keep = 1.0 - flags
    upad = jnp.pad(u, ((KCONV - 1, 0), (0, 0)))
    kpad = jnp.pad(keep, ((KCONV - 1, 0), (0, 0)), constant_values=1.0)
    conv = conv_b + conv_w[0] * u
    alive = jnp.ones_like(keep)
    for shift_k in range(1, KCONV):
        alive = alive * kpad[KCONV - shift_k:KCONV - shift_k + TOKENS]
        conv = conv + conv_w[shift_k] * upad[KCONV - 1 - shift_k:KCONV - 1 - shift_k + TOKENS] * alive
    c = low(conv)
    blocks = c.reshape(TOKENS, R // BLK, BLK)
    apre = low_back(jnp.einsum('thk,hkj->thj', blocks, wa, precision=high).reshape(TOKENS, R) + ba)
    ipre = low_back(jnp.einsum('thk,hkj->thj', blocks, wi, precision=high).reshape(TOKENS, R) + bi)
    rgate = jax.nn.sigmoid(apre)
    igate = jax.nn.sigmoid(ipre)
    loga = -lru_power * rgate * jax.nn.softplus(-lam)
    mult = flags + keep * jnp.sqrt(-jnp.expm1(2.0 * loga))
    carry = jnp.exp(loga) * keep
    drive = mult * igate * c
    unused, state = lax.associative_scan(link, (carry, drive), axis=0)
    gated = low(y * state)
    rec = low_back(jnp.dot(gated, wo, precision=high))
    x2 = x + rec
    n2 = low(rms_scale(x2, g2))
    gpre = low_back(jnp.dot(n2, wg, precision=high))
    upm = low_back(jnp.dot(n2, wu, precision=high))
    hid = low(gelu_tanh(gpre) * upm)
    return x2 + jnp.dot(hid, wd, precision=high)

def reference(stream, prescale, gelumat, gelubias, lrumat, lrubias, convtaps, convbias, recgates, recbias, inpgates, inpbias, lambdas, outmat, midscale, gatemat, upmatrix, downmat, resets, cotangent):
    flags = resets.astype(jnp.float32)[:, None]
    f32 = jnp.float32
    prims = (stream.astype(f32), prescale, gelumat.astype(f32), gelubias, lrumat.astype(f32), lrubias, convtaps, convbias, recgates.astype(f32), recbias, inpgates.astype(f32), inpbias, lambdas, outmat.astype(f32), midscale, gatemat.astype(f32), upmatrix.astype(f32), downmat.astype(f32))

    def closed(*values):
        return forward(*values, flags)
    result, pullback = jax.vjp(closed, *prims)
    grads = pullback(cotangent.astype(f32))
    return (result.astype(jnp.bfloat16), grads[0].astype(jnp.bfloat16), grads[1], grads[2], grads[3], grads[4], grads[5], grads[6], grads[7], grads[8], grads[9], grads[10], grads[11], grads[12], grads[13], grads[14], grads[15], grads[16], grads[17])
```

```python
import functools
import jax
import jax.numpy as jnp
from jax import lax
from jax.experimental import pallas as pl
from jax.experimental.pallas import tpu as pltpu
from jax.sharding import PartitionSpec as P

f32 = jnp.float32
bf16 = jnp.bfloat16
EPS = 1e-06
POWER = 8.0
HALO = 16
SEGS = 8
MIB = 1 << 20
ROOT = 0.7978845608028654
CUBE = 0.044715


def dot(a, b):
    return jnp.dot(a, b, preferred_element_type=f32)


def dot_nt(a, b):
    return lax.dot_general(a, b, (((1,), (1,)), ((), ())), preferred_element_type=f32)


def dot_tn(a, b):
    return lax.dot_general(a, b, (((0,), (0,)), ((), ())), preferred_element_type=f32)


def whole(shape):
    return pl.BlockSpec(shape, lambda *i: (0,) * len(shape))


def params(mib):
    return pltpu.CompilerParams(
        dimension_semantics=("arbitrary",), vmem_limit_bytes=mib * MIB
    )


def sds(shape, dtype):
    return jax.ShapeDtypeStruct(shape, dtype)


def one_minus_exp(z):
    s = 1.0 - z * (1.0 / 8.0)
    for n in (7.0, 6.0, 5.0, 4.0, 3.0, 2.0):
        s = 1.0 - (z * (1.0 / n)) * s
    return z * s


def gelu(v):
    th = jnp.tanh(ROOT * (v + CUBE * v * v * v))
    return 0.5 * v * (1.0 + th)


def gelu_both(v):
    sq = v * v
    th = jnp.tanh(ROOT * v * (1.0 + CUBE * sq))
    half = 0.5 * (1.0 + th)
    slope = half + 0.5 * v * (1.0 - th * th) * (ROOT * (1.0 + 3.0 * CUBE * sq))
    return v * half, slope


def recur_kernel(
    x_ref, xe_ref, m_ref, wy_ref, wx_ref, vec_ref, g1_ref, wai_ref,
    n1_ref, ypre_ref, u_ref, c_ref, carry_ref, r_ref, i_ref, h_ref, p_ref, end_ref, ue_ref,
    uext, cbuf, dbuf, hs, ps, run,
):
    tb, width = x_ref.shape
    chan = wy_ref.shape[1]
    length = tb // SEGS
    b = pl.program_id(0)
    vec = lambda k: vec_ref[k : k + 1, :]

    def norm(v):
        v = v.astype(f32)
        ms = jnp.mean(v * v, axis=-1, keepdims=True)
        return (v * lax.rsqrt(ms + EPS) * g1_ref[...]).astype(bf16)

    @pl.when(b == 0)
    def _():
        ne = norm(xe_ref[:, :width])
        ue = (dot(ne, wx_ref[...]) + vec(1)).astype(bf16).astype(f32)
        ue = ue * xe_ref[:, width : width + 1].astype(f32)
        uext[:HALO, :] = ue
        ue_ref[...] = ue
        run[0:1, :] = jnp.ones((1, chan), f32)
        run[1:2, :] = jnp.zeros((1, chan), f32)

    @pl.when(b > 0)
    def _():
        uext[:HALO, :] = uext[tb : tb + HALO, :]

    n1 = norm(x_ref[...])
    n1_ref[...] = n1
    u = (dot(n1, wx_ref[...]) + vec(1)).astype(bf16)
    u_ref[...] = u
    uext[HALO:, :] = u.astype(f32)
    ypre_ref[...] = dot(n1, wy_ref[...]) + vec(0)
    keep = m_ref[:, 0:1]
    alive2 = m_ref[:, 1:2]
    alive3 = m_ref[:, 2:3]
    side = wai_ref.shape[1]
    for k in range(chan // side):
        ln = slice(k * side, (k + 1) * side)
        v = lambda j: vec_ref[j : j + 1, ln]
        conv = v(6) + v(2) * uext[HALO:, ln]
        conv = conv + v(3) * uext[HALO - 1 : HALO - 1 + tb, ln] * keep
        conv = conv + v(4) * uext[HALO - 2 : HALO - 2 + tb, ln] * alive2
        conv = conv + v(5) * uext[HALO - 3 : HALO - 3 + tb, ln] * alive3
        c = conv.astype(bf16)
        c_ref[:, ln] = c
        g = dot(c, wai_ref[k])
        r = jax.nn.sigmoid(g[:, :side] + v(7))
        i = jax.nn.sigmoid(g[:, side:] + v(8))
        r_ref[:, ln] = r
        i_ref[:, ln] = i
        decay = r * v(9)
        mult = (1.0 - keep) + keep * jnp.sqrt(one_minus_exp(2.0 * decay))
        carry = jnp.exp(-decay) * keep
        carry_ref[:, ln] = carry
        cbuf[k] = carry
        dbuf[k] = mult * i * c.astype(f32)
    blocks = chan // 128
    hh = [jnp.zeros((SEGS, 128), f32) for _ in range(blocks)]
    pp = [jnp.ones((SEGS, 128), f32) for _ in range(blocks)]
    for j in range(length):
        rows = pl.ds(j, SEGS, stride=length)
        for k in range(blocks):
            a = cbuf[k, rows, :]
            hh[k] = a * hh[k] + dbuf[k, rows, :]
            pp[k] = a * pp[k]
            hs[k, rows, :] = hh[k]
            ps[k, rows, :] = pp[k]
    for k in range(blocks):
        ln = slice(k * 128, (k + 1) * 128)
        prow = run[0:1, ln]
        hrow = run[1:2, ln]
        for s in range(SEGS):
            rows = slice(s * length, (s + 1) * length)
            pseg = ps[k, rows, :]
            h_ref[rows, ln] = hs[k, rows, :] + pseg * hrow
            p_ref[rows, ln] = pseg * prow
            hrow = hh[k][s : s + 1, :] + pp[k][s : s + 1, :] * hrow
            prow = pp[k][s : s + 1, :] * prow
        run[0:1, ln] = prow
        run[1:2, ln] = hrow
        end_ref[0:1, ln] = prow
        end_ref[1:2, ln] = hrow


def recur(x, xe, masks, wy, wx, vec, g1, wai, tb):
    rows, width = x.shape
    chan = wy.shape[1]
    rowspec = lambda w: pl.BlockSpec((tb, w), lambda b: (b, 0))
    act = [(width, bf16), (chan, f32), (chan, bf16), (chan, bf16)] + [(chan, f32)] * 5
    return pl.pallas_call(
        recur_kernel,
        grid=(rows // tb,),
        in_specs=[
            rowspec(width), whole(xe.shape), rowspec(masks.shape[1]), whole(wy.shape),
            whole(wx.shape), whole(vec.shape), whole(g1.shape), whole(wai.shape),
        ],
        out_specs=[rowspec(w) for w, _ in act] + [whole((2, chan)), whole((HALO, chan))],
        out_shape=[sds((rows, w), d) for w, d in act]
        + [sds((2, chan), f32), sds((HALO, chan), f32)],
        scratch_shapes=[
            pltpu.VMEM((tb + HALO, chan), f32),
            *[pltpu.VMEM((chan // 128, tb, 128), f32)] * 4,
            pltpu.VMEM((2, chan), f32),
        ],
        compiler_params=params(40),
        name="recur",
    )(x, xe, masks, wy, wx, vec, g1, wai)


def entering(ends_ref, mine, backward):
    count = ends_ref.shape[0]
    total = jnp.zeros_like(ends_ref[0, 1:2, :])
    for s in range(count - 1):
        at = count - 1 - s if backward else s
        new = ends_ref[at, 0:1, :] * total + ends_ref[at, 1:2, :]
        inside = at > mine if backward else at < mine
        total = jnp.where(inside, new, total)
    return total


def out_kernel(mine_ref, h_ref, p_ref, ypre_ref, ends_ref, wo_ref, *rest):
    state_ref, gl_ref, part_ref = rest[-3:]
    into = entering(ends_ref, mine_ref[0], False)
    state = h_ref[...] + p_ref[...] * into
    state_ref[...] = state
    gl = (gelu(ypre_ref[...]) * state).astype(bf16)
    gl_ref[...] = gl
    part_ref[...] = dot(gl, wo_ref[...]).astype(bf16)


SMEM = pl.BlockSpec(memory_space=pltpu.SMEM)
ANY = pl.BlockSpec(memory_space=pl.ANY)


def chunk_call(kernel, at, tb, chunked, fixed, outs, carried, extra_outs, mib, name, scratch=()):
    rows = chunked[0].shape[0]
    spec = lambda w: pl.BlockSpec((tb, w), lambda *i: (at, 0))
    carried = [] if carried is None else list(carried)
    base = len(fixed) + len(chunked)
    ins = [SMEM if a.dtype == jnp.int32 else whole(a.shape) for a in fixed]
    return pl.pallas_call(
        kernel,
        grid=(1,),
        in_specs=ins + [spec(a.shape[1]) for a in chunked] + [ANY] * len(carried),
        out_specs=[spec(w) for w, _ in outs] + [whole(s) for s, _ in extra_outs],
        out_shape=[sds((rows, w), d) for w, d in outs] + [sds(s, d) for s, d in extra_outs],
        scratch_shapes=list(scratch),
        input_output_aliases={base + k: k for k in range(len(carried))},
        compiler_params=params(mib),
        name=name,
    )(*fixed, *chunked, *carried)


def out_chunk(at, tb, mine, h, p, ypre, ends, wo, carried):
    def kernel(mine_ref, ends_ref, wo_ref, h_ref, p_ref, ypre_ref, *rest):
        out_kernel(mine_ref, h_ref, p_ref, ypre_ref, ends_ref, wo_ref, *rest)

    chan, width = wo.shape
    return chunk_call(
        kernel, at, tb, [h, p, ypre], [mine, ends, wo], [(chan, f32), (chan, bf16)],
        carried, [((tb, width), bf16)], 24, "out_proj",
    )


def slopes_kernel(
    mine_ref, ends_ref, vec_ref, r_ref, i_ref, carry_ref, c_ref, state_ref, before_ref, m_ref,
    a_ref, b_ref, d_ref, g_ref, sext,
):
    tb = r_ref.shape[0]
    b = pl.program_id(0)
    sext[8:, :] = state_ref[...]
    sext[:8, :] = before_ref[...]

    @pl.when(b == 0)
    def _():
        sext[7:8, :] = entering(ends_ref, mine_ref[0], False)

    keep = m_ref[:, 0:1]
    sp = vec_ref[9:10, :]
    r = r_ref[...]
    i = i_ref[...]
    c = c_ref[...].astype(f32)
    m2 = one_minus_exp(2.0 * (r * sp))
    m = jnp.sqrt(m2)
    mult = (1.0 - keep) + keep * m
    prior = sext[7 : 7 + tb, :]
    grad = prior * carry_ref[...] - i * c * keep * (1.0 - m2) / m
    gr = grad * r
    g_ref[...] = gr
    a_ref[...] = -gr * sp * (1.0 - r)
    mi = mult * i
    b_ref[...] = mi * c * (1.0 - i)
    d_ref[...] = mi


def slopes(mine, ends, vec, r, i, carry, c, state, masks, tb):
    rows, chan = r.shape
    spec = lambda w: pl.BlockSpec((tb, w), lambda b: (b, 0))
    before = pl.BlockSpec((8, chan), lambda b: (jnp.maximum(b * (tb // 8) - 1, 0), 0))
    return pl.pallas_call(
        slopes_kernel,
        grid=(rows // tb,),
        in_specs=[SMEM, whole(ends.shape), whole(vec.shape)]
        + [spec(chan)] * 5
        + [before, spec(masks.shape[1])],
        out_specs=[spec(chan)] * 4,
        out_shape=[sds((rows, chan), f32)] * 4,
        scratch_shapes=[pltpu.VMEM((tb + 8, chan), f32)],
        compiler_params=params(24),
        name="slopes",
    )(mine, ends, vec, r, i, carry, c, state, state, masks)


def pick(mid_ref, t_ref, far_ref):
    mid = mid_ref[0] == 1
    return jnp.where(mid, t_ref[...], far_ref[...])


def mlp_kernel(
    mid_ref, t_ref, far_ref, g2_ref, wg_ref, wu_ref, wd_ref, x_ref, cot_ref, *rest,
):
    rec_ref, n2_ref, hid_ref, dg_ref, du_ref, mpart_ref, dpart_ref, n2s, macc, dacc = rest[-10:]
    f = pl.program_id(0)

    @pl.when(f == 0)
    def _():
        rec = pick(mid_ref, t_ref, far_ref)
        rec_ref[...] = rec
        x2 = x_ref[...].astype(f32) + rec.astype(f32)
        ms = jnp.mean(x2 * x2, axis=-1, keepdims=True)
        n2 = (x2 * lax.rsqrt(ms + EPS) * g2_ref[...]).astype(bf16)
        n2s[...] = n2
        n2_ref[...] = n2

    n2 = n2s[...]
    wd = wd_ref[...]
    wg = wg_ref[...]
    wu = wu_ref[...]
    gpre = dot(n2, wg)
    up = dot(n2, wu)
    dh = dot_nt(cot_ref[...], wd)
    act, slope = gelu_both(gpre)
    hid = (act * up).astype(bf16)
    dg = (dh * up * slope).astype(bf16)
    du = (dh * act).astype(bf16)
    hid_ref[...] = hid
    dg_ref[...] = dg
    du_ref[...] = du
    mp = dot(hid, wd)
    dp = dot_nt(dg, wg) + dot_nt(du, wu)
    last = pl.num_programs(0) - 1

    @pl.when(f == 0)
    def _():
        macc[...] = mp
        dacc[...] = dp

    @pl.when((f > 0) & (f < last))
    def _():
        macc[...] += mp
        dacc[...] += dp

    @pl.when(f == last)
    def _():
        mpart_ref[...] = (macc[...] + mp).astype(bf16)
        dpart_ref[...] = (dacc[...] + dp).astype(bf16)


def mlp_chunk(at, tb, mid, t, far, g2, wg, wu, wd, x, cot, carried, fb):
    rows, width = x.shape
    hidden = wg.shape[1]
    row = lambda w: pl.BlockSpec((tb, w), lambda f: (at, 0))
    col = pl.BlockSpec((tb, fb), lambda f: (at, f))
    carried = [] if carried is None else list(carried)
    return pl.pallas_call(
        mlp_kernel,
        grid=(hidden // fb,),
        in_specs=[
            SMEM, whole(t.shape), whole(far.shape), whole(g2.shape),
            pl.BlockSpec((width, fb), lambda f: (0, f)), pl.BlockSpec((width, fb), lambda f: (0, f)),
            pl.BlockSpec((fb, width), lambda f: (f, 0)), row(width), row(width),
        ]
        + [ANY] * len(carried),
        out_specs=[row(width), row(width), col, col, col, whole((tb, width)), whole((tb, width))],
        out_shape=[sds((rows, width), bf16)] * 2
        + [sds((rows, hidden), bf16)] * 3
        + [sds((tb, width), bf16)] * 2,
        scratch_shapes=[
            pltpu.VMEM((tb, width), bf16), pltpu.VMEM((tb, width), f32), pltpu.VMEM((tb, width), f32),
        ],
        input_output_aliases={9 + k: k for k in range(len(carried))},
        compiler_params=params(40),
        name="mlp",
    )(mid, t, far, g2, wg, wu, wd, x, cot, *carried)


def back_kernel(
    mid_ref, t_ref, far_ref, g2_ref, wo_ref, run_ref,
    x_ref, rec_ref, cot_ref, state_ref, ypre_ref, carry_ref, *rest,
):
    dx2_ref, drec_ref, branch_ref, adj_ref, q_ref, end_ref, dg2_ref, cbuf, dbuf, al, ql = rest[-11:]
    tb = x_ref.shape[0]
    chan = wo_ref.shape[0]
    length = tb // SEGS
    dn = pick(mid_ref, t_ref, far_ref).astype(f32)
    x2 = x_ref[...].astype(f32) + rec_ref[...].astype(f32)
    inv = lax.rsqrt(jnp.mean(x2 * x2, axis=-1, keepdims=True) + EPS)
    hat = x2 * inv
    dh = dn * hat
    dg2_ref[...] = jnp.sum(dh, axis=0, keepdims=True)
    g2 = g2_ref[...]
    dot_mean = jnp.mean(dh * g2, axis=-1, keepdims=True)
    dx2 = cot_ref[...].astype(f32) + inv * (dn * g2 - hat * dot_mean)
    dx2_ref[...] = dx2
    drec = dx2.astype(bf16)
    drec_ref[...] = drec
    dgl = dot_nt(drec, wo_ref[...])
    y, slope = gelu_both(ypre_ref[...])
    branch_ref[...] = (dgl * state_ref[...] * slope).astype(bf16)
    dstate = dgl * y
    blocks = chan // 128
    for k in range(blocks):
        ln = slice(k * 128, (k + 1) * 128)
        cbuf[k] = carry_ref[:, ln]
        dbuf[k] = dstate[:, ln]
    ee = [jnp.zeros((SEGS, 128), f32) for _ in range(blocks)]
    qq = [jnp.ones((SEGS, 128), f32) for _ in range(blocks)]
    for j in range(length - 1, -1, -1):
        rows = pl.ds(j, SEGS, stride=length)
        for k in range(blocks):
            a = cbuf[k, rows, :]
            adj = dbuf[k, rows, :] + ee[k]
            al[k, rows, :] = adj
            ql[k, rows, :] = qq[k]
            ee[k] = a * adj
            qq[k] = a * qq[k]
    for k in range(blocks):
        ln = slice(k * 128, (k + 1) * 128)
        qrow = run_ref[0:1, ln]
        erow = run_ref[1:2, ln]
        for s in range(SEGS - 1, -1, -1):
            rows = slice(s * length, (s + 1) * length)
            qseg = ql[k, rows, :]
            adj_ref[rows, ln] = al[k, rows, :] + qseg * erow
            q_ref[rows, ln] = qseg * qrow
            qend = qq[k][s : s + 1, :]
            erow = ee[k][s : s + 1, :] + qend * erow
            qrow = qend * qrow
        end_ref[0:1, ln] = qrow
        end_ref[1:2, ln] = erow


def back_chunk(at, tb, mid, t, far, g2, wo, run, x, rec, cot, state, ypre, carry, carried):
    chan, width = wo.shape
    return chunk_call(
        back_kernel, at, tb, [x, rec, cot, state, ypre, carry], [mid, t, far, g2, wo, run],
        [(width, f32), (width, bf16), (chan, bf16), (chan, f32), (chan, f32)], carried,
        [((2, chan), f32), ((1, width), f32)], 40, "mid_back",
        [pltpu.VMEM((chan // 128, tb, 128), f32)] * 4,
    )


def gates_kernel(
    mine_ref, ends_ref, vec_ref, wai_ref, ue_ref,
    adj_ref, q_ref, a_ref, b_ref, d_ref, g_ref, c_ref, u_ref, before_ref, m_ref, branch_ref,
    du_ref, tail_ref, edge_ref, gw_ref, sums_ref, uext, e1, e2, e3,
):
    tb, chan = adj_ref.shape
    step = pl.program_id(0)
    steps = pl.num_programs(0)
    side = wai_ref.shape[1]
    vec = lambda k: vec_ref[k : k + 1, :]

    @pl.when(step == 0)
    def _():
        for e in (e1, e2, e3):
            e[tb:, :] = jnp.zeros((8, chan), f32)
        gw_ref[...] = jnp.zeros_like(gw_ref)
        sums_ref[...] = jnp.zeros_like(sums_ref)

    @pl.when(step > 0)
    def _():
        for e in (e1, e2, e3):
            e[tb:, :] = e[:8, :]

    uext[HALO:, :] = u_ref[...].astype(f32)

    @pl.when(step == steps - 1)
    def _():
        uext[:HALO, :] = ue_ref[...]

    @pl.when(step < steps - 1)
    def _():
        uext[:HALO, :] = before_ref[...].astype(f32)

    into = entering(ends_ref, mine_ref[0], True)
    keep = m_ref[:, 0:1]
    alive2 = m_ref[:, 1:2]
    alive3 = m_ref[:, 2:3]

    def add(k, ln, value):
        sums_ref[k : k + 1, ln] += jnp.sum(value, axis=0, keepdims=True)

    for k in range(chan // side):
        ln = slice(k * side, (k + 1) * side)
        adj = adj_ref[:, ln] + q_ref[:, ln] * into[:, ln]
        add(2, ln, adj * g_ref[:, ln])
        da = (adj * a_ref[:, ln]).astype(bf16)
        di = (adj * b_ref[:, ln]).astype(bf16)
        add(0, ln, da.astype(f32))
        add(1, ln, di.astype(f32))
        both = jnp.concatenate([da, di], axis=1)
        gw_ref[k] += dot_tn(c_ref[:, ln], both)
        dconv = adj * d_ref[:, ln] + dot_nt(both, wai_ref[k])
        add(3, ln, dconv)
        add(4, ln, dconv * uext[HALO:, ln])
        mk = dconv * keep
        e1[:tb, ln] = mk
        add(5, ln, mk * uext[HALO - 1 : HALO - 1 + tb, ln])
        mk = dconv * alive2
        e2[:tb, ln] = mk
        add(6, ln, mk * uext[HALO - 2 : HALO - 2 + tb, ln])
        mk = dconv * alive3
        e3[:tb, ln] = mk
        add(7, ln, mk * uext[HALO - 3 : HALO - 3 + tb, ln])
        v = lambda j: vec_ref[j : j + 1, ln]
        du = v(2) * dconv + v(3) * e1[1 : 1 + tb, ln]
        du = du + v(4) * e2[2 : 2 + tb, ln] + v(5) * e3[3 : 3 + tb, ln]
        low = du.astype(bf16)
        du_ref[:, ln] = low
        add(8, ln, low.astype(f32))
        add(9, ln, branch_ref[:, ln].astype(f32))

        @pl.when(step == 0)
        def _():
            tail_ref[:, ln] = du[tb - HALO :, :]
            sums_ref[8:9, ln] -= jnp.sum(low[tb - HALO :, :].astype(f32), axis=0, keepdims=True)

    @pl.when(step == steps - 1)
    def _():
        edge_ref[...] = jnp.zeros_like(edge_ref)
        edge_ref[5:6, :] = vec(5) * e3[0:1, :]
        edge_ref[6:7, :] = vec(4) * e2[0:1, :] + vec(5) * e3[1:2, :]
        edge_ref[7:8, :] = vec(3) * e1[0:1, :] + vec(4) * e2[1:2, :] + vec(5) * e3[2:3, :]
        sums_ref[2:3, :] = sums_ref[2:3, :] * vec(10)


def gates_back(mine, ends, vec, wai, ue, adj, q, slope4, c, u, masks, branch, tb):
    rows, chan = adj.shape
    n = rows // tb
    spec = lambda w: pl.BlockSpec((tb, w), lambda b: (n - 1 - b, 0))
    per = tb // HALO
    before = pl.BlockSpec((HALO, chan), lambda b: (jnp.maximum((n - 1 - b) * per - 1, 0), 0))
    blocks, side, two = wai.shape
    return pl.pallas_call(
        gates_kernel,
        grid=(n,),
        in_specs=[SMEM, whole(ends.shape), whole(vec.shape), whole(wai.shape), whole(ue.shape)]
        + [spec(chan)] * 8
        + [before, spec(masks.shape[1]), spec(chan)],
        out_specs=[
            spec(chan), whole((HALO, chan)), whole((8, chan)), whole(wai.shape), whole((16, chan)),
        ],
        out_shape=[
            sds((rows, chan), bf16), sds((HALO, chan), f32), sds((8, chan), f32),
            sds(wai.shape, f32), sds((16, chan), f32),
        ],
        scratch_shapes=[pltpu.VMEM((tb + HALO, chan), f32)] + [pltpu.VMEM((tb + 8, chan), f32)] * 3,
        compiler_params=params(40),
        name="gates_back",
    )(mine, ends, vec, wai, ue, adj, q, *slope4, c, u, u, masks, branch)


def in_kernel(wy_ref, wx_ref, x_ref, branch_ref, du_ref, part_ref, dg1_ref):
    part = dot_nt(branch_ref[...], wy_ref[...]) + dot_nt(du_ref[...], wx_ref[...])
    part_ref[...] = part.astype(bf16)
    x = x_ref[...].astype(f32)
    inv = lax.rsqrt(jnp.mean(x * x, axis=-1, keepdims=True) + EPS)
    dg1_ref[...] = jnp.sum(part * (x * inv), axis=0, keepdims=True)


def in_chunk(at, tb, wy, wx, x, branch, du):
    width = x.shape[1]
    return chunk_call(
        in_kernel, at, tb, [x, branch, du], [wy, wx], [], None,
        [((tb, width), bf16), ((1, width), f32)], 32, "in_back",
    )


def result_kernel(mid_ref, t_ref, far_ref, x_ref, rec_ref, *rest):
    total = x_ref[...].astype(f32) + rec_ref[...].astype(f32)
    rest[-1][...] = (total + pick(mid_ref, t_ref, far_ref).astype(f32)).astype(bf16)


def result_chunk(at, tb, mid, t, far, x, rec, carried):
    return chunk_call(
        result_kernel, at, tb, [x, rec], [mid, t, far], [(x.shape[1], bf16)], carried, [], 24,
        "result",
    )


def last_kernel(mid_ref, t_ref, far_ref, g1_ref, x_ref, dx2_ref, *rest):
    dn = pick(mid_ref, t_ref, far_ref).astype(f32) * g1_ref[...]
    x = x_ref[...].astype(f32)
    inv = lax.rsqrt(jnp.mean(x * x, axis=-1, keepdims=True) + EPS)
    hat = x * inv
    mean = jnp.mean(dn * hat, axis=-1, keepdims=True)
    rest[-1][...] = (dx2_ref[...] + inv * (dn - hat * mean)).astype(bf16)


def last_chunk(at, tb, mid, t, far, g1, x, dx2, carried):
    return chunk_call(
        last_kernel, at, tb, [x, dx2], [mid, t, far, g1], [(x.shape[1], bf16)], carried, [], 24,
        "stream_grad",
    )


def weights_kernel(pairs, offset, *refs):
    out_ref = refs[-1]
    j = pl.program_id(0)
    ins = refs[: 2 * len(pairs)]
    for k in range(len(pairs)):

        @pl.when(j == k)
        def _(k=k):
            at = pl.ds(pl.multiple_of(pl.program_id(1) * out_ref.shape[0], 128), out_ref.shape[0])
            out_ref[...] = dot_tn(ins[2 * k][:, at], ins[2 * k + 1][...]).astype(bf16)


def weights(pairs, db, columns, offset=0, carried=None):
    height = pairs[0][0].shape[1]
    wide = pairs[0][1].shape[1]
    flat = [a for pair in pairs for a in pair]
    once = lambda a: pl.BlockSpec(a.shape, lambda j, i: (0, 0), pipeline_mode=pl.Buffered(1))
    extra = [] if carried is None else [carried]
    return pl.pallas_call(
        functools.partial(weights_kernel, pairs, offset),
        grid=(len(pairs), height // db),
        in_specs=[once(a) for a in flat] + [ANY] * len(extra),
        out_specs=pl.BlockSpec((db, wide), lambda j, i: (i, j + offset)),
        out_shape=sds((height, columns), bf16),
        input_output_aliases={len(flat): 0} if extra else {},
        compiler_params=pltpu.CompilerParams(
            dimension_semantics=("arbitrary", "arbitrary"), vmem_limit_bytes=48 * MIB
        ),
        name="weight_grads",
    )(*flat, *extra)


class Fold:
    def __init__(self, axis):
        self.axis = axis
        self.n = lax.axis_size(axis)
        me = lax.axis_index(axis)
        n = self.n
        self.line = n == 4
        mid = ((me == 1) | (me == 2)) if self.line else me >= 0
        self.mid = mid.astype(jnp.int32)[None]

    def __call__(self, part):
        if not self.line:
            total = lax.psum(part, self.axis)
            return total, total
        got = lax.ppermute(part, self.axis, [(0, 1), (3, 2)])
        s = part + got
        got = lax.ppermute(s, self.axis, [(1, 2), (2, 1)])
        t = s + got
        far = lax.ppermute(t, self.axis, [(1, 0), (2, 3)])
        return t, far


def everyone(value, axis):
    n = lax.axis_size(axis)
    if n & (n - 1):
        return lax.psum(value, axis)
    bit = 1
    while bit < n:
        got = lax.ppermute(value, axis, [(i, i ^ bit) for i in range(n)])
        value = (value.astype(f32) + got.astype(f32)).astype(value.dtype)
        bit *= 2
    return value


def body(
    x, prescale, wy, by, wx, bx, conv_w, conv_b, wa, ba, wi, bi, lam, wo, midscale, wg, wu, wd,
    resets, cot,
):
    rows, width = x.shape
    chan = wy.shape[1]
    hidden = wg.shape[1]
    blocks, side = wa.shape[:2]
    n_seq = lax.axis_size("seq")
    mine = lax.axis_index("seq").astype(jnp.int32)[None]
    fold = Fold("head")
    mid = fold.mid
    tb = 256
    chunks = rows // tb
    order = list(range(chunks - 1, -1, -1))

    g1 = prescale[None]
    g2 = midscale[None]
    keep = 1.0 - resets.astype(f32)
    k1 = jnp.concatenate([jnp.ones((1,), f32), keep[:-1]])
    k2 = jnp.concatenate([jnp.ones((2,), f32), keep[:-2]])
    masks = jnp.stack([keep, keep * k1, keep * k1 * k2, keep], axis=1)
    tail1 = keep[rows - 1]
    tail2 = tail1 * keep[rows - 2]
    zero = jnp.zeros((HALO - 3,), f32)
    edge_mask = jnp.concatenate([zero, jnp.stack([tail2, tail1, jnp.ones((), f32)])])[:, None]
    packed = jnp.concatenate(
        [x[rows - HALO :], jnp.broadcast_to(edge_mask, (HALO, 128)).astype(bf16)], axis=1
    )
    forward = [(i, i + 1) for i in range(n_seq - 1)]
    backward = [(i + 1, i) for i in range(n_seq - 1)]
    xe = lax.ppermute(packed, "seq", forward)
    vec = jnp.concatenate(
        [
            by[None], bx[None], conv_w, conv_b[None], ba[None], bi[None],
            POWER * jax.nn.softplus(-lam)[None], POWER * jax.nn.sigmoid(-lam)[None],
            jnp.zeros((5, chan), f32),
        ],
        axis=0,
    )
    wai = jnp.concatenate([wa, wi], axis=2)

    n1, ypre, u, c, carry, r, i, h, p, end, ue = recur(x, xe, masks, wy, wx, vec, g1, wai, tb)
    ends = lax.all_gather(end, "seq")

    kept = None
    rec_sum = {}
    for at in order:
        *kept, part = out_chunk(at, tb, mine, h, p, ypre, ends, wo, kept)
        rec_sum[at] = fold(part)
    state, gl = kept
    slope4 = slopes(mine, ends, vec, r, i, carry, c, state, masks, tb)

    kept = None
    mlp_part, n2_sum = {}, {}
    for at in order:
        *kept, mlp_part[at], part = mlp_chunk(
            at, tb, mid, *rec_sum[at], g2, wg, wu, wd, x, cot, kept, 384
        )
        n2_sum[at] = fold(part)
    rec, n2, hid, dg, du2 = kept
    big = weights([(n2, dg), (n2, du2), (cot, hid)], 512, 3 * hidden)
    big = lax.psum_scatter(big, "seq", scatter_dimension=0, tiled=True)

    kept = None
    run = jnp.concatenate([jnp.ones((1, chan), f32), jnp.zeros((1, chan), f32)])
    d_g2 = 0.0
    for at in order:
        *kept, run, dg2 = back_chunk(
            at, tb, mid, *n2_sum[at], g2, wo, run, x, rec, cot, state, ypre, carry, kept
        )
        d_g2 = d_g2 + dg2
    dx2, drec, branch, adj, q = kept
    ends_back = lax.all_gather(run, "seq")

    mlp_sum = {at: fold(mlp_part[at]) for at in order}

    du, tail, edge, gw, sums = gates_back(
        mine, ends_back, vec, wai, ue, adj, q, slope4, c, u, masks, branch, tb
    )
    returned = lax.ppermute(edge, "seq", backward)
    patch = tail + jnp.concatenate([jnp.zeros((HALO - 8, chan), f32), returned]) * edge_mask
    patch = patch.astype(bf16)
    du = lax.dynamic_update_slice(du, patch, (rows - HALO, 0))
    sums = sums.at[8].add(jnp.sum(patch.astype(f32), axis=0))

    d_g1 = 0.0
    n1_sum = {}
    for at in range(chunks):
        part, dg1 = in_chunk(at, tb, wy, wx, x, branch, du)
        d_g1 = d_g1 + dg1
        n1_sum[at] = fold(part)
    small = weights([(n1, branch), (n1, du), (drec, gl)], 512, 3 * chan)
    small = lax.psum_scatter(small, "seq", scatter_dimension=0, tiled=True)

    stack = jnp.concatenate([gw.reshape(blocks * side, 2 * side), sums.reshape(-1, 2 * side)])
    stack = everyone(stack.astype(bf16), "seq").astype(f32)
    gw = stack[: blocks * side].reshape(blocks, side, 2 * side)
    sums = stack[blocks * side :].reshape(16, chan)
    gains = jnp.concatenate([d_g1, d_g2 * (1.0 / fold.n)])
    gains = lax.psum(gains, ("seq", "head"))
    piece = width // n_seq
    gains = lax.dynamic_slice(gains, (0, mine[0] * piece), (2, piece))

    result = None
    for at in order:
        result = result_chunk(at, tb, mid, *mlp_sum[at], x, rec, result)
    d_x = None
    for at in range(chunks):
        d_x = last_chunk(at, tb, mid, *n1_sum[at], g1, x, dx2, d_x)

    big = big.astype(f32)
    small = small.astype(f32)
    return (
        result[0], d_x[0], gains[0], small[:, :chan], sums[9], small[:, chan : 2 * chan], sums[8],
        sums[4:8], sums[3], gw[:, :, :side], sums[0], gw[:, :, side:], sums[1], sums[2],
        small[:, 2 * chan :].T, gains[1], big[:, :hidden], big[:, hidden : 2 * hidden],
        big[:, 2 * hidden :].T,
    )


def solution(mesh):
    col, row, both = P(None, "head"), P("head", None), P("seq", "head")
    head, seq, cube = P("head"), P("seq"), P("head", None, None)
    tokens = P("seq", None)
    in_specs = (
        tokens, P(), col, head, col, head, col, head, cube, head, cube, head, head, row, P(), col,
        col, row, seq, tokens,
    )
    out_specs = (
        tokens, tokens, seq, both, head, both, head, col, head, cube, head, cube, head, head,
        P("head", "seq"), seq, both, both, P("head", "seq"),
    )
    return jax.shard_map(body, mesh=mesh, in_specs=in_specs, out_specs=out_specs, check_vma=False)
```

```python
import functools
import jax
import jax.numpy as jnp
from jax import lax
from jax.experimental import pallas as pl
from jax.experimental.pallas import tpu as pltpu
from jax.sharding import PartitionSpec as P

f32 = jnp.float32
bf16 = jnp.bfloat16
EPS = 1e-06
POWER = 8.0
HALO = 16
SEGS = 8
MIB = 1 << 20
ROOT = 0.7978845608028654
CUBE = 0.044715


def dot(a, b):
    return jnp.dot(a, b, preferred_element_type=f32)


def dot_nt(a, b):
    return lax.dot_general(a, b, (((1,), (1,)), ((), ())), preferred_element_type=f32)


def dot_tn(a, b):
    return lax.dot_general(a, b, (((0,), (0,)), ((), ())), preferred_element_type=f32)


def in_hbm(a):
    return pltpu.with_memory_space_constraint(a, pltpu.HBM)


def in_vmem(a):
    return pltpu.with_memory_space_constraint(a, pltpu.VMEM)


def whole(shape):
    return pl.BlockSpec(shape, lambda *i: (0,) * len(shape))


SMEM = pl.BlockSpec(memory_space=pltpu.SMEM)
ANY = pl.BlockSpec(memory_space=pl.ANY)
VMEM = pl.BlockSpec(memory_space=pltpu.VMEM)


def sds(shape, dtype):
    return jax.ShapeDtypeStruct(shape, dtype)


def one_minus_exp(z):
    s = 1.0 - z * (1.0 / 8.0)
    for n in (7.0, 6.0, 5.0, 4.0, 3.0, 2.0):
        s = 1.0 - (z * (1.0 / n)) * s
    return z * s


def gelu(v):
    th = jnp.tanh(ROOT * (v + CUBE * v * v * v))
    return 0.5 * v * (1.0 + th)


def gelu_both(v):
    sq = v * v
    th = jnp.tanh(ROOT * v * (1.0 + CUBE * sq))
    half = 0.5 * (1.0 + th)
    slope = half + 0.5 * v * (1.0 - th * th) * (ROOT * (1.0 + 3.0 * CUBE * sq))
    return v * half, slope


class Chain:
    def __init__(self):
        self.token = None

    def __call__(
        self, kernel, args, in_specs, outs, name, grid=(1,), carried=None, scratch=(), mib=32,
        cost=None,
    ):
        args, in_specs = list(args), list(in_specs)
        aliases = {}
        for k, a in enumerate(carried or []):
            aliases[len(args)] = k
            args.append(in_hbm(a))
            in_specs.append(ANY)
        n_in = len(args)
        if self.token is not None:
            args.append(self.token)
            in_specs.append(ANY)
        n_all = len(args)
        n_out = len(outs)
        used = n_in - len(aliases)

        def wrapped(*refs):
            refs[n_all + n_out][...] = jnp.zeros((8, 128), f32)
            kernel(*refs[:used], *refs[n_all : n_all + n_out], *refs[n_all + n_out + 1 :])

        *got, self.token = pl.pallas_call(
            wrapped,
            grid=grid,
            in_specs=in_specs,
            out_specs=[out[0] for out in outs] + [whole((8, 128))],
            out_shape=[out[3] if len(out) > 3 else sds(*out[1:3]) for out in outs]
            + [sds((8, 128), f32)],
            scratch_shapes=list(scratch),
            input_output_aliases=aliases,
            compiler_params=pltpu.CompilerParams(
                dimension_semantics=("arbitrary",) * len(grid), vmem_limit_bytes=mib * MIB
            ),
            cost_estimate=cost and pl.CostEstimate(flops=cost, bytes_accessed=1, transcendentals=0),
            name=name,
        )(*args)
        return got


def pinned(spec, shape, dtype):
    return spec, shape, dtype, pltpu.HBM(shape, dtype)


def rows_at(off, tb, width):
    return pl.BlockSpec((pl.Element(tb), pl.Element(width)), lambda *i: (off, 0))


def proj_kernel(x_ref, wy_ref, wx_ref, by_ref, bx_ref, g1_ref, n1_ref, ypre_ref, u_ref):
    n1 = norm(x_ref[...], g1_ref[...])
    n1_ref[...] = n1
    u_ref[...] = (dot(n1, wx_ref[...]) + bx_ref[...]).astype(bf16)
    ypre_ref[...] = dot(n1, wy_ref[...]) + by_ref[...]


def norm(v, gain):
    v = v.astype(f32)
    ms = jnp.mean(v * v, axis=-1, keepdims=True)
    return (v * lax.rsqrt(ms + EPS) * gain).astype(bf16)


def project(chain, x, wy, wx, by, bx, g1, tb):
    rows, width = x.shape
    chan = wy.shape[1]
    spec = lambda w: pl.BlockSpec((tb, w), lambda b: (b, 0))
    return chain(
        proj_kernel, [in_hbm(x), in_hbm(wy), in_hbm(wx), by, bx, g1],
        [spec(width)] + [whole(a.shape) for a in (wy, wx, by, bx, g1)],
        [
            pinned(spec(width), (rows, width), bf16), (spec(chan), (rows, chan), f32),
            (spec(chan), (rows, chan), bf16),
        ],
        "project", grid=(rows // tb,),
    )


def spread_masks(m_ref, kext, keep_row):
    tb = m_ref.shape[0]
    k0 = kext[HALO : HALO + tb, 0:1]
    k1 = kext[HALO - 1 : HALO - 1 + tb, 0:1]
    k2 = kext[HALO - 2 : HALO - 2 + tb, 0:1]
    return k0, k0 * k1, k0 * k1 * k2


def recur_kernel(
    mine_ref, xe_ref, wx_ref, bx_ref, g1_ref, wa_ref, wi_ref, conv_w_ref, conv_b_ref, ba_ref,
    bi_ref, lam_ref, u_ref, flag_ref,
    c_ref, carry_ref, r_ref, i_ref, h_ref, p_ref, end_ref, ue_ref, ke_ref, vec_ref,
    uext, kext, cbuf, dbuf, hs, ps, run,
):
    tb, chan = u_ref.shape
    width = wx_ref.shape[0]
    length = tb // SEGS
    b = pl.program_id(0)

    @pl.when(b == 0)
    def _():
        inside = jnp.where(mine_ref[0] > 0, 1.0, 0.0)
        ne = norm(xe_ref[:, :width], g1_ref[...])
        ue = (dot(ne, wx_ref[...]) + bx_ref[...]).astype(bf16).astype(f32) * inside
        uext[:HALO, :] = ue
        ue_ref[...] = ue
        ke = 1.0 - xe_ref[:, width : width + 128].astype(f32)
        kext[:HALO, :] = ke
        ke_ref[...] = ke
        run[0:1, :] = jnp.ones((1, chan), f32)
        run[1:2, :] = jnp.zeros((1, chan), f32)
        vec_ref[0:4, :] = conv_w_ref[...]
        e = jnp.exp(-lam_ref[...])
        soft = e * (1.0 - e * (0.5 - e * (1.0 / 3.0 - e * (0.25 - e * (0.2 - e * (1.0 / 6.0))))))
        vec_ref[4:5, :] = POWER * soft
        vec_ref[5:6, :] = POWER * e / (1.0 + e)
        vec_ref[6:8, :] = jnp.zeros((2, chan), f32)

    @pl.when(b > 0)
    def _():
        uext[:HALO, :] = uext[tb : tb + HALO, :]
        kext[:HALO, :] = kext[tb : tb + HALO, :]

    uext[HALO:, :] = u_ref[...].astype(f32)
    kext[HALO:, :] = jnp.broadcast_to(1.0 - flag_ref[...].astype(f32), (tb, 128))
    keep, alive2, alive3 = spread_masks(flag_ref, kext, None)
    side = wa_ref.shape[1]
    for k in range(chan // side):
        ln = slice(k * side, (k + 1) * side)
        tap = lambda j: conv_w_ref[j : j + 1, ln]
        conv = conv_b_ref[:, ln] + tap(0) * uext[HALO:, ln]
        conv = conv + tap(1) * uext[HALO - 1 : HALO - 1 + tb, ln] * keep
        conv = conv + tap(2) * uext[HALO - 2 : HALO - 2 + tb, ln] * alive2
        conv = conv + tap(3) * uext[HALO - 3 : HALO - 3 + tb, ln] * alive3
        c = conv.astype(bf16)
        c_ref[:, ln] = c
        r = jax.nn.sigmoid(dot(c, wa_ref[k]) + ba_ref[:, ln])
        i = jax.nn.sigmoid(dot(c, wi_ref[k]) + bi_ref[:, ln])
        r_ref[:, ln] = r
        i_ref[:, ln] = i
        decay = r * vec_ref[4:5, ln]
        mult = (1.0 - keep) + keep * jnp.sqrt(one_minus_exp(2.0 * decay))
        carry = jnp.exp(-decay) * keep
        carry_ref[:, ln] = carry
        cbuf[k] = carry
        dbuf[k] = mult * i * c.astype(f32)
    blocks = chan // 128
    hh = [jnp.zeros((SEGS, 128), f32) for _ in range(blocks)]
    pp = [jnp.ones((SEGS, 128), f32) for _ in range(blocks)]
    for j in range(length):
        rows = pl.ds(j, SEGS, stride=length)
        for k in range(blocks):
            a = cbuf[k, rows, :]
            hh[k] = a * hh[k] + dbuf[k, rows, :]
            pp[k] = a * pp[k]
            hs[k, rows, :] = hh[k]
            ps[k, rows, :] = pp[k]
    for k in range(blocks):
        ln = slice(k * 128, (k + 1) * 128)
        prow = run[0:1, ln]
        hrow = run[1:2, ln]
        for s in range(SEGS):
            rows = slice(s * length, (s + 1) * length)
            pseg = ps[k, rows, :]
            h_ref[rows, ln] = hs[k, rows, :] + pseg * hrow
            p_ref[rows, ln] = pseg * prow
            hrow = hh[k][s : s + 1, :] + pp[k][s : s + 1, :] * hrow
            prow = pp[k][s : s + 1, :] * prow
        run[0:1, ln] = prow
        run[1:2, ln] = hrow
        end_ref[0:1, ln] = prow
        end_ref[1:2, ln] = hrow


def recur(chain, mine, xe, wx, bx, g1, wa, wi, conv_w, conv_b, ba, bi, lam, u, flags, tb):
    rows, chan = u.shape
    spec = lambda w: pl.BlockSpec((tb, w), lambda b: (b, 0))
    fixed = [xe, wx, bx, g1, wa, wi, conv_w, conv_b, ba, bi, lam]
    full = lambda shape: (whole(shape), shape, f32)
    return chain(
        recur_kernel, [mine, *fixed, u, flags],
        [SMEM] + [whole(a.shape) for a in fixed] + [spec(chan), spec(1)],
        [pinned(spec(chan), (rows, chan), bf16)]
        + [pinned(spec(chan), (rows, chan), f32)] * 3
        + [(spec(chan), (rows, chan), f32)] * 2
        + [full((2, chan)), full((HALO, chan)), full((HALO, 128)), full((8, chan))],
        "recur", grid=(rows // tb,),
        scratch=[
            pltpu.VMEM((tb + HALO, chan), f32),
            pltpu.VMEM((tb + HALO, 128), f32),
            *[pltpu.VMEM((chan // 128, tb, 128), f32)] * 4,
            pltpu.VMEM((2, chan), f32),
        ],
    )


def entering(ends_ref, mine, backward):
    count = ends_ref.shape[0]
    total = jnp.zeros_like(ends_ref[0, 1:2, :])
    for s in range(count - 1):
        at = count - 1 - s if backward else s
        new = ends_ref[at, 0:1, :] * total + ends_ref[at, 1:2, :]
        inside = at > mine if backward else at < mine
        total = jnp.where(inside, new, total)
    return total


def out_kernel(mine_ref, ends_ref, wo_ref, h_ref, p_ref, ypre_ref, state_ref, gl_ref, part_ref):
    into = entering(ends_ref, mine_ref[0], False)
    state = h_ref[...] + p_ref[...] * into
    state_ref[...] = state
    gl = (gelu(ypre_ref[...]) * state).astype(bf16)
    gl_ref[...] = gl
    part_ref[...] = dot(gl, wo_ref[...]).astype(bf16)


def chunk_call(chain, kernel, chunk, fixed, chunked, outs, own, name, free=False, held=(), **more):
    off, tb = chunk
    rows = chunked[0].shape[0]
    ins = [SMEM if a.dtype == jnp.int32 else whole(a.shape) for a in fixed]
    ins += [VMEM] * len(held)
    return chain(
        kernel, list(fixed) + [in_vmem(a) for a in held] + [a if free else in_hbm(a) for a in chunked],
        ins + [rows_at(off, tb, a.shape[1]) for a in chunked],
        [pinned(rows_at(off, tb, w), (rows, w), d) for w, d in outs]
        + [(whole(s), s, d) for s, d in own],
        name, **more,
    )


def out_chunk(chain, chunk, mine, h, p, ypre, ends, wo, carried):
    chan, width = wo.shape
    return chunk_call(
        chain, out_kernel, chunk, [mine, ends, wo], [h, p, ypre], [(chan, f32), (chan, bf16)],
        [((chunk[1], width), bf16)], "out_proj", carried=carried, free=True,
    )


def slopes_kernel(
    mine_ref, ends_ref, vec_ref, r_ref, i_ref, carry_ref, c_ref, state_ref, before_ref, flag_ref,
    a_ref, b_ref, d_ref, g_ref, sext,
):
    tb = r_ref.shape[0]
    b = pl.program_id(0)
    sext[8:, :] = state_ref[...]
    sext[:8, :] = before_ref[...]

    @pl.when(b == 0)
    def _():
        sext[7:8, :] = entering(ends_ref, mine_ref[0], False)

    keep = 1.0 - flag_ref[...].astype(f32)
    sp = vec_ref[4:5, :]
    r = r_ref[...]
    i = i_ref[...]
    c = c_ref[...].astype(f32)
    m2 = one_minus_exp(2.0 * (r * sp))
    m = jnp.sqrt(m2)
    mult = (1.0 - keep) + keep * m
    prior = sext[7 : 7 + tb, :]
    grad = prior * carry_ref[...] - i * c * keep * (1.0 - m2) / m
    gr = grad * r
    g_ref[...] = gr
    a_ref[...] = -gr * sp * (1.0 - r)
    mi = mult * i
    b_ref[...] = mi * c * (1.0 - i)
    d_ref[...] = mi


def slopes(chain, mine, ends, vec, r, i, carry, c, state, flags, tb):
    rows, chan = r.shape
    spec = lambda w: pl.BlockSpec((tb, w), lambda b: (b, 0))
    before = pl.BlockSpec((8, chan), lambda b: (jnp.maximum(b * (tb // 8) - 1, 0), 0))
    return chain(
        slopes_kernel,
        [mine, ends, vec] + [in_hbm(a) for a in (r, i, carry, c, state, state)] + [flags],
        [SMEM, whole(ends.shape), whole(vec.shape)] + [spec(chan)] * 5 + [before, spec(1)],
        [pinned(spec(chan), (rows, chan), f32)] * 4,
        "slopes", grid=(rows // tb,), scratch=[pltpu.VMEM((tb + 8, chan), f32)],
    )


def pick(mid_ref, t_ref, far_ref):
    mid = mid_ref[0] == 1
    return jnp.where(mid, t_ref[...], far_ref[...])


def mlp_kernel(
    mid_ref, g2_ref, t_ref, far_ref, wg_ref, wu_ref, wd_ref, x_ref, cot_ref,
    rec_ref, n2_ref, hid_ref, dg_ref, du_ref, mpart_ref, dpart_ref,
):
    rec = pick(mid_ref, t_ref, far_ref)
    rec_ref[...] = rec
    n2 = norm(x_ref[...].astype(f32) + rec.astype(f32), g2_ref[...])
    n2_ref[...] = n2
    gpre = dot(n2, wg_ref[...])
    up = dot(n2, wu_ref[...])
    dh = dot_nt(cot_ref[...], wd_ref[...])
    act, slope = gelu_both(gpre)
    hid = (act * up).astype(bf16)
    dg = (dh * up * slope).astype(bf16)
    du = (dh * act).astype(bf16)
    hid_ref[...] = hid
    dg_ref[...] = dg
    du_ref[...] = du
    dpart_ref[...] = (dot_nt(dg, wg_ref[...]) + dot_nt(du, wu_ref[...])).astype(bf16)
    mpart_ref[...] = dot(hid, wd_ref[...]).astype(bf16)


def mlp_chunk(chain, chunk, mid, t, far, g2, wg, wu, wd, x, cot, carried):
    width = x.shape[1]
    hidden = wg.shape[1]
    tb = chunk[1]
    return chunk_call(
        chain, mlp_kernel, chunk, [mid, g2, t, far], [x, cot],
        [(width, bf16)] * 2 + [(hidden, bf16)] * 3, [((tb, width), bf16)] * 2, "mlp",
        carried=carried, mib=36, held=(wg, wu, wd),
    )


def back_kernel(
    mid_ref, t_ref, far_ref, g2_ref, wo_ref, run_ref,
    x_ref, rec_ref, cot_ref, state_ref, ypre_ref, carry_ref,
    dx2_ref, drec_ref, branch_ref, adj_ref, q_ref, end_ref, dg2_ref, cbuf, dbuf, al, ql,
):
    tb = x_ref.shape[0]
    chan = wo_ref.shape[0]
    length = tb // SEGS
    dn = pick(mid_ref, t_ref, far_ref).astype(f32)
    x2 = x_ref[...].astype(f32) + rec_ref[...].astype(f32)
    inv = lax.rsqrt(jnp.mean(x2 * x2, axis=-1, keepdims=True) + EPS)
    hat = x2 * inv
    dh = dn * hat
    dg2_ref[...] = jnp.sum(dh, axis=0, keepdims=True)
    g2 = g2_ref[...]
    dot_mean = jnp.mean(dh * g2, axis=-1, keepdims=True)
    dx2 = cot_ref[...].astype(f32) + inv * (dn * g2 - hat * dot_mean)
    dx2_ref[...] = dx2
    drec = dx2.astype(bf16)
    drec_ref[...] = drec
    dgl = dot_nt(drec, wo_ref[...])
    y, slope = gelu_both(ypre_ref[...])
    branch_ref[...] = (dgl * state_ref[...] * slope).astype(bf16)
    dstate = dgl * y
    blocks = chan // 128
    for k in range(blocks):
        ln = slice(k * 128, (k + 1) * 128)
        cbuf[k] = carry_ref[:, ln]
        dbuf[k] = dstate[:, ln]
    ee = [jnp.zeros((SEGS, 128), f32) for _ in range(blocks)]
    qq = [jnp.ones((SEGS, 128), f32) for _ in range(blocks)]
    for j in range(length - 1, -1, -1):
        rows = pl.ds(j, SEGS, stride=length)
        for k in range(blocks):
            a = cbuf[k, rows, :]
            adj = dbuf[k, rows, :] + ee[k]
            al[k, rows, :] = adj
            ql[k, rows, :] = qq[k]
            ee[k] = a * adj
            qq[k] = a * qq[k]
    for k in range(blocks):
        ln = slice(k * 128, (k + 1) * 128)
        qrow = run_ref[0:1, ln]
        erow = run_ref[1:2, ln]
        for s in range(SEGS - 1, -1, -1):
            rows = slice(s * length, (s + 1) * length)
            qseg = ql[k, rows, :]
            adj_ref[rows, ln] = al[k, rows, :] + qseg * erow
            q_ref[rows, ln] = qseg * qrow
            qend = qq[k][s : s + 1, :]
            erow = ee[k][s : s + 1, :] + qend * erow
            qrow = qend * qrow
        end_ref[0:1, ln] = qrow
        end_ref[1:2, ln] = erow


def back_chunk(chain, chunk, mid, t, far, g2, wo, run, x, rec, cot, state, ypre, carry, carried):
    chan, width = wo.shape
    return chunk_call(
        chain, back_kernel, chunk, [mid, t, far, g2, wo, run], [x, rec, cot, state, ypre, carry],
        [(width, f32), (width, bf16), (chan, bf16), (chan, f32), (chan, f32)],
        [((2, chan), f32), ((1, width), f32)], "mid_back", carried=carried,
        scratch=[pltpu.VMEM((chan // 128, chunk[1], 128), f32)] * 4,
    )


def gates_kernel(
    mine_ref, ends_ref, vec_ref, wa_ref, wi_ref, ue_ref, ke_ref,
    adj_ref, q_ref, a_ref, b_ref, d_ref, g_ref, c_ref, u_ref, before_ref, flag_ref, flag_before_ref,
    branch_ref, du_ref, tail_ref, edge_ref, gwa_ref, gwi_ref, sums_ref, uext, kext, e1, e2, e3,
):
    tb, chan = adj_ref.shape
    step = pl.program_id(0)
    steps = pl.num_programs(0)
    side = wa_ref.shape[1]
    vec = lambda k: vec_ref[k : k + 1, :]

    @pl.when(step == 0)
    def _():
        for e in (e1, e2, e3):
            e[tb:, :] = jnp.zeros((8, chan), f32)
        gwa_ref[...] = jnp.zeros_like(gwa_ref)
        gwi_ref[...] = jnp.zeros_like(gwi_ref)
        sums_ref[...] = jnp.zeros_like(sums_ref)

    @pl.when(step > 0)
    def _():
        for e in (e1, e2, e3):
            e[tb:, :] = e[:8, :]

    uext[HALO:, :] = u_ref[...].astype(f32)
    kext[HALO:, :] = jnp.broadcast_to(1.0 - flag_ref[...].astype(f32), (tb, 128))

    @pl.when(step == steps - 1)
    def _():
        uext[:HALO, :] = ue_ref[...]
        kext[:HALO, :] = ke_ref[...]

    @pl.when(step < steps - 1)
    def _():
        uext[:HALO, :] = before_ref[...].astype(f32)
        kext[:HALO, :] = jnp.broadcast_to(1.0 - flag_before_ref[...].astype(f32), (HALO, 128))

    into = entering(ends_ref, mine_ref[0], True)
    keep, alive2, alive3 = spread_masks(flag_ref, kext, None)

    def add(k, ln, value):
        sums_ref[k : k + 1, ln] += jnp.sum(value, axis=0, keepdims=True)

    for k in range(chan // side):
        ln = slice(k * side, (k + 1) * side)
        adj = adj_ref[:, ln] + q_ref[:, ln] * into[:, ln]
        add(2, ln, adj * g_ref[:, ln])
        da = (adj * a_ref[:, ln]).astype(bf16)
        di = (adj * b_ref[:, ln]).astype(bf16)
        add(0, ln, da.astype(f32))
        add(1, ln, di.astype(f32))
        gwa_ref[k] += dot_tn(c_ref[:, ln], da)
        gwi_ref[k] += dot_tn(c_ref[:, ln], di)
        dconv = adj * d_ref[:, ln] + dot_nt(da, wa_ref[k]) + dot_nt(di, wi_ref[k])
        add(3, ln, dconv)
        add(4, ln, dconv * uext[HALO:, ln])
        mk = dconv * keep
        e1[:tb, ln] = mk
        add(5, ln, mk * uext[HALO - 1 : HALO - 1 + tb, ln])
        mk = dconv * alive2
        e2[:tb, ln] = mk
        add(6, ln, mk * uext[HALO - 2 : HALO - 2 + tb, ln])
        mk = dconv * alive3
        e3[:tb, ln] = mk
        add(7, ln, mk * uext[HALO - 3 : HALO - 3 + tb, ln])
        v = lambda j: vec_ref[j : j + 1, ln]
        du = v(0) * dconv + v(1) * e1[1 : 1 + tb, ln]
        du = du + v(2) * e2[2 : 2 + tb, ln] + v(3) * e3[3 : 3 + tb, ln]
        low = du.astype(bf16)
        du_ref[:, ln] = low
        add(8, ln, low.astype(f32))
        add(9, ln, branch_ref[:, ln].astype(f32))

        @pl.when(step == 0)
        def _():
            tail_ref[:, ln] = du[tb - HALO :, :]
            sums_ref[8:9, ln] -= jnp.sum(low[tb - HALO :, :].astype(f32), axis=0, keepdims=True)

    @pl.when(step == steps - 1)
    def _():
        edge_ref[...] = jnp.zeros_like(edge_ref)
        edge_ref[5:6, :] = vec(3) * e3[0:1, :]
        edge_ref[6:7, :] = vec(2) * e2[0:1, :] + vec(3) * e3[1:2, :]
        edge_ref[7:8, :] = vec(1) * e1[0:1, :] + vec(2) * e2[1:2, :] + vec(3) * e3[2:3, :]
        sums_ref[2:3, :] = sums_ref[2:3, :] * vec(5)


def gates_back(chain, mine, ends, vec, wa, wi, ue, ke, adj, q, slope4, c, u, flags, branch, tb):
    rows, chan = adj.shape
    n = rows // tb
    spec = lambda w: pl.BlockSpec((tb, w), lambda b: (n - 1 - b, 0))
    per = tb // HALO
    before = lambda w: pl.BlockSpec((HALO, w), lambda b: (jnp.maximum((n - 1 - b) * per - 1, 0), 0))
    full = lambda shape: (whole(shape), shape, f32)
    fixed = [ends, vec, wa, wi, ue, ke]
    return chain(
        gates_kernel,
        [mine, *fixed] + [in_hbm(a) for a in (adj, q, *slope4, c, u, u)] + [flags, flags]
        + [in_hbm(branch)],
        [SMEM] + [whole(a.shape) for a in fixed] + [spec(chan)] * 8
        + [before(chan), spec(1), before(1), spec(chan)],
        [
            pinned(spec(chan), (rows, chan), bf16), full((HALO, chan)), full((8, chan)), full(wa.shape),
            full(wi.shape), full((16, chan)),
        ],
        "gates_back", grid=(n,), mib=40, cost=LONG_G,
        scratch=[pltpu.VMEM((tb + HALO, chan), f32), pltpu.VMEM((tb + HALO, 128), f32)]
        + [pltpu.VMEM((tb + 8, chan), f32)] * 3,
    )


def in_kernel(wy_ref, wx_ref, x_ref, branch_ref, du_ref, part_ref, dg1_ref):
    part = dot_nt(branch_ref[...], wy_ref[...]) + dot_nt(du_ref[...], wx_ref[...])
    part_ref[...] = part.astype(bf16)
    x = x_ref[...].astype(f32)
    inv = lax.rsqrt(jnp.mean(x * x, axis=-1, keepdims=True) + EPS)
    dg1_ref[...] = jnp.sum(part * (x * inv), axis=0, keepdims=True)


def in_chunk(chain, chunk, wy, wx, x, branch, du):
    width = x.shape[1]
    return chunk_call(
        chain, in_kernel, chunk, [wy, wx], [x, branch, du], [],
        [((chunk[1], width), bf16), ((1, width), f32)], "in_back",
    )


def result_kernel(mid_ref, t_ref, far_ref, x_ref, rec_ref, out_ref):
    total = x_ref[...].astype(f32) + rec_ref[...].astype(f32)
    out_ref[...] = (total + pick(mid_ref, t_ref, far_ref).astype(f32)).astype(bf16)


def result_chunk(chain, chunk, mid, t, far, x, rec, carried):
    return chunk_call(
        chain, result_kernel, chunk, [mid, t, far], [x, rec], [(x.shape[1], bf16)], [], "result",
        carried=carried,
    )


def last_kernel(mid_ref, t_ref, far_ref, g1_ref, x_ref, dx2_ref, out_ref):
    dn = pick(mid_ref, t_ref, far_ref).astype(f32) * g1_ref[...]
    x = x_ref[...].astype(f32)
    inv = lax.rsqrt(jnp.mean(x * x, axis=-1, keepdims=True) + EPS)
    hat = x * inv
    mean = jnp.mean(dn * hat, axis=-1, keepdims=True)
    out_ref[...] = (dx2_ref[...] + inv * (dn - hat * mean)).astype(bf16)


def last_chunk(chain, chunk, mid, t, far, g1, x, dx2, carried, cost):
    return chunk_call(
        chain, last_kernel, chunk, [mid, t, far, g1], [x, dx2], [(x.shape[1], bf16)], [],
        "stream_grad", carried=carried, cost=cost,
    )


def weight_grad(chain, a, b, at, columns, db, carried):
    height, wide = a.shape[1], b.shape[1]

    def kernel(a_ref, b_ref, out_ref):
        out_ref[...] = dot_tn(a_ref[...], b_ref[...]).astype(bf16)

    rows = a.shape[0]
    return chain(
        kernel, [in_hbm(a), in_hbm(b)],
        [pl.BlockSpec((rows, db), lambda i: (0, i)), whole(b.shape)],
        [pinned(pl.BlockSpec((db, wide), lambda i: (i, at)), (height, columns), bf16)],
        "weight_grad", grid=(height // db,), carried=carried, mib=24,
    )


def widen(chain, total, name):
    rows, columns = total.shape
    third = columns // 3

    def kernel(t_ref, a_ref, b_ref, c_ref):
        a_ref[...] = t_ref[:, :third].astype(f32)
        b_ref[...] = t_ref[:, third : 2 * third].astype(f32)
        c_ref[...] = t_ref[:, 2 * third :].astype(f32).T

    shapes = [(rows, third), (rows, third), (third, rows)]
    return chain(
        kernel, [total], [whole(total.shape)], [(whole(s), s, f32) for s in shapes], name
    )


def add_pair(chain, a, b):
    def kernel(a_ref, b_ref, out_ref):
        out_ref[...] = (a_ref[...].astype(f32) + b_ref[...].astype(f32)).astype(out_ref.dtype)

    return chain(
        kernel, [a, b], [whole(a.shape), whole(b.shape)], [(whole(a.shape), a.shape, a.dtype)],
        "hop_sum",
    )[0]


class Fold:
    def __init__(self, chain, axis):
        self.chain = chain
        self.axis = axis
        self.line = lax.axis_size(axis) == 4

    def start(self, part):
        self.part = part
        if self.line:
            self.got = lax.ppermute(part, self.axis, [(0, 1), (3, 2)])
        else:
            self.t = self.far = lax.psum(part, self.axis)

    def swap(self):
        if self.line:
            self.part = add_pair(self.chain, self.part, self.got)
            self.got = lax.ppermute(self.part, self.axis, [(1, 2), (2, 1)])

    def back(self):
        if self.line:
            self.t = add_pair(self.chain, self.part, self.got)
            self.far = lax.ppermute(self.t, self.axis, [(1, 0), (2, 3)])

    def pair(self):
        return self.t, self.far


class Exchange:
    def __init__(self, chain, value, axis):
        self.chain, self.axis, self.value = chain, axis, value
        self.n = lax.axis_size(axis)
        self.bit = 1
        if self.n & (self.n - 1):
            self.value = lax.psum(value, axis)
            self.bit = self.n
        self.send()

    def send(self):
        if self.bit < self.n:
            route = [(i, i ^ self.bit) for i in range(self.n)]
            self.got = lax.ppermute(self.value, self.axis, route)

    def step(self):
        if self.bit < self.n:
            self.value = add_pair(self.chain, self.value, self.got)
            self.bit *= 2
            self.send()

    def finish(self):
        while self.bit < self.n:
            self.step()
        return self.value


def split(sizes):
    chunks, off = [], 0
    for size in sizes:
        chunks.append((off, size))
        off += size
    return chunks


def body(
    x, prescale, wy, by, wx, bx, conv_w, conv_b, wa, ba, wi, bi, lam, wo, midscale, wg, wu, wd,
    resets, cot,
):
    rows, width = x.shape
    chan = wy.shape[1]
    hidden = wg.shape[1]
    blocks, side = wa.shape[:2]
    n_seq = lax.axis_size("seq")
    n_head = lax.axis_size("head")
    mine = lax.axis_index("seq").astype(jnp.int32)[None]
    me = lax.axis_index("head")
    mid = ((me == 1) | (me == 2)).astype(jnp.int32)[None]
    chain = Chain()
    tb = 256
    sizes = FIRST if sum(FIRST) == rows else [rows // 4] * 4
    one = split(sizes)[::-1]
    sizes = LAST if sum(LAST) == rows else [rows // 4] * 4
    two = split(sizes)

    g1, g2 = prescale[None], midscale[None]
    flags = resets[:, None]
    packed = jnp.concatenate(
        [x[rows - HALO :], jnp.broadcast_to(flags[rows - HALO :], (HALO, 128)).astype(bf16)], axis=1
    )
    forward = [(i, i + 1) for i in range(n_seq - 1)]
    backward = [(i + 1, i) for i in range(n_seq - 1)]
    xe = lax.ppermute(packed, "seq", forward)
    n1, ypre, u = project(chain, x, wy, wx, by[None], bx[None], g1, tb)
    c, carry, r, i, h, p, end, ue, ke, vec = recur(
        chain, mine, xe, wx, bx[None], g1, wa, wi, conv_w, conv_b[None], ba[None], bi[None],
        lam[None], u, flags, tb,
    )
    ends = lax.all_gather(end, "seq")

    n = len(one)
    rec_f = [Fold(chain, "head") for _ in one]
    n2_f = [Fold(chain, "head") for _ in one]
    n1_f = [Fold(chain, "head") for _ in two]
    mlp_f = [Fold(chain, "head") for _ in one]
    d = {}

    kept = None
    for k in range(n):
        *kept, part = out_chunk(chain, one[k], mine, h, p, ypre, ends, wo, kept)
        rec_f[k].start(part)
    state, gl = kept
    slope4 = slopes(chain, mine, ends, vec, r, i, carry, c, state, flags, tb)

    def mlp(k):
        *d["mlp"], d["mp", k], dp = mlp_chunk(
            chain, one[k], mid, *rec_f[k].pair(), g2, wg, wu, wd, x, cot, d.get("mlp")
        )
        n2_f[k].start(dp)

    def back(k):
        run = d.get("run")
        if run is None:
            run = jnp.concatenate([jnp.ones((1, chan), f32), jnp.zeros((1, chan), f32)])
        *d["back"], d["run"], dg2 = back_chunk(
            chain, one[k], mid, *n2_f[k].pair(), g2, wo, run, x, d["mlp"][0], cot, state, ypre,
            carry, d.get("back"),
        )
        d["g2"] = d.get("g2", 0.0) + dg2

    def big(k):
        rec, n2, hid, dg, du2 = d["mlp"]
        a, b = ((n2, dg), (n2, du2), (cot, hid))[k]
        d["big"] = weight_grad(chain, a, b, k, 3 * hidden, 512, d.get("big"))

    def start_mlp(k):
        mlp_f[k].start(d["mp", k])

    def sum_mlp():
        totals = lax.psum([d["mp", k] for k in range(n)], "head")
        for k in range(n):
            mlp_f[k].t = mlp_f[k].far = totals[k]

    def result(k):
        d["result"] = result_chunk(
            chain, one[k], mid, *mlp_f[k].pair(), x, d["mlp"][0], d.get("result")
        )

    def scatter():
        d["big_sum"] = lax.psum_scatter(d["big"][0], "seq", scatter_dimension=0, tiled=True)

    def gather():
        d["ends"] = lax.all_gather(d["run"], "seq")

    def gates():
        dx2, drec, branch, adj, q = d["back"]
        d["du"], d["tail"], edge, d["gwa"], d["gwi"], d["sums"] = gates_back(
            chain, mine, d["ends"], vec, wa, wi, ue, ke, adj, q, slope4, c, u, flags, branch, tb
        )
        d["edge"] = lax.ppermute(edge, "seq", backward)

    def patched():
        patch = d["tail"] + jnp.concatenate([jnp.zeros((HALO - 8, chan), f32), d["edge"]])
        patch = patch.astype(bf16)
        d["du"] = lax.dynamic_update_slice(d["du"], patch, (rows - HALO, 0))
        d["sums"] = d["sums"].at[8].add(jnp.sum(patch.astype(f32), axis=0))

    def inner(k):
        part, dg1 = in_chunk(chain, two[k], wy, wx, x, d["back"][2], d["du"])
        d["g1"] = d.get("g1", 0.0) + dg1
        n1_f[k].start(part)

    def lru_weights(k):
        dx2, drec, branch, adj, q = d["back"]
        a, b = ((n1, branch), (n1, d["du"]), (drec, gl))[k]
        d["small"] = weight_grad(chain, a, b, k, 3 * chan, 512, d.get("small"))

    def scatter_small():
        d["small_sum"] = lax.psum_scatter(d["small"][0], "seq", scatter_dimension=0, tiled=True)

    def stacked():
        gains = jnp.concatenate([d["g1"], d["g2"] * (1.0 / n_head)])
        pieces = [d[name].reshape(-1, side) for name in ("gwa", "gwi", "sums")]
        pieces.append(gains.reshape(-1, side))
        cuts = [0]
        for piece in pieces:
            cuts.append(cuts[-1] + piece.shape[0])
        d["cuts"] = cuts
        stack = jnp.concatenate(pieces + [jnp.zeros((-cuts[-1] % 16, side), f32)]).astype(bf16)
        d["stack"] = Exchange(chain, stack, "seq")

    def stack_step():
        d["stack"].step()

    def head_start():
        d["total"] = d["stack"].finish()
        d["gains"] = Exchange(chain, d["total"][d["cuts"][3] :], "head")

    def head_step():
        d["gains"].step()

    def widen_big():
        d["big_out"] = widen(chain, d["big_sum"], "mlp_grads")

    def widen_small():
        d["small_out"] = widen(chain, d["small_sum"], "lru_grads")

    def last(k):
        d["last"] = last_chunk(
            chain, two[k], mid, *n1_f[k].pair(), g1, x, d["back"][0], d.get("last"),
            LONG if k == len(two) - 1 else None,
        )

    calls = {
        "Rs": lambda k: rec_f[k].swap(), "Rb": lambda k: rec_f[k].back(), "M": mlp,
        "Ns": lambda k: n2_f[k].swap(), "Nb": lambda k: n2_f[k].back(), "B": back, "W": big,
        "I": inner, "X": patched, "V": lru_weights, "As": lambda k: n1_f[k].swap(),
        "Ab": lambda k: n1_f[k].back(), "L": last, "P": start_mlp, "sum_mlp": sum_mlp, "T": result,
        "Ps": lambda k: mlp_f[k].swap(), "Pb": lambda k: mlp_f[k].back(), "scatter": scatter,
        "gather": gather, "gates": gates, "scatter_small": scatter_small, "stack": stacked,
        "stack_step": stack_step, "head": head_start, "head_step": head_step, "big": widen_big,
        "small": widen_small,
    }
    for line in ORDER:
        for step in line.split():
            name = step.rstrip("0123456789")
            calls[name](*([int(step[len(name) :])] if step != name else []))

    g_y, g_x, g_o = d["small_out"]
    g_gate, g_up, g_down = d["big_out"]
    cuts = d["cuts"]
    total = d["total"].astype(f32)
    gains = d["gains"].finish()[: cuts[4] - cuts[3]].astype(f32).reshape(2, width)
    gwa = total[: cuts[1]].reshape(wa.shape)
    gwi = total[cuts[1] : cuts[2]].reshape(wi.shape)
    sums = total[cuts[2] : cuts[3]].reshape(16, chan)
    piece = width // n_seq
    gains = lax.dynamic_slice(gains, (0, mine[0] * piece), (2, piece))
    return (
        d["result"][0], d["last"][0], gains[0], g_y, sums[9], g_x, sums[8], sums[4:8], sums[3],
        gwa, sums[0], gwi, sums[1], sums[2], g_o, gains[1], g_gate, g_up, g_down,
    )


LONG = 3 * 10**10
LONG_G = 10**13
FIRST = [256, 256, 256, 256]
LAST = [256, 256, 256, 256]

ORDER = [
    "Rs0 Rs1 Rb0 Rs2", "Rb1 M0 P0 Rs3", "Rb2 M1 P1 Ns0", "Rb3 M2 P2 Ns1", "Nb0 M3 P3 Ns2",
    "Nb1 W0 B0 W1", "Ns3 Ps0 Nb2 W2", "scatter B1 Nb3 Ps1", "Pb0 B2 Ps2 Pb1",
    "B3 gather gates Ps3", "Pb2 T0 I0 I1", "I2 T1 X I3", "Pb3 T2 As0 V0", "V2 stack As1 Ab0",
    "V1 scatter_small T3 stack_step", "As2 Ab1 L0 stack_step", "As3 Ab2 L1 stack_step",
    "head Ab3 L2 head_step", "head_step L3 big small",
]


def solution(mesh):
    col, row, both = P(None, "head"), P("head", None), P("seq", "head")
    head, seq, cube = P("head"), P("seq"), P("head", None, None)
    tokens = P("seq", None)
    in_specs = (
        tokens, P(), col, head, col, head, col, head, cube, head, cube, head, head, row, P(), col,
        col, row, seq, tokens,
    )
    out_specs = (
        tokens, tokens, seq, both, head, both, head, col, head, cube, head, cube, head, head,
        P("head", "seq"), seq, both, both, P("head", "seq"),
    )
    return jax.shard_map(body, mesh=mesh, in_specs=in_specs, out_specs=out_specs, check_vma=False)
```

```python
import functools
import jax
import jax.numpy as jnp
from jax import lax
from jax.experimental import pallas as pl
from jax.experimental.pallas import tpu as pltpu
from jax.sharding import PartitionSpec as P

f32 = jnp.float32
bf16 = jnp.bfloat16
EPS = 1e-06
POWER = 8.0
HALO = 16
SEGS = 8
MIB = 1 << 20
ROOT = 0.7978845608028654
CUBE = 0.044715


def dot(a, b):
    return jnp.dot(a, b, preferred_element_type=f32)


def dot_nt(a, b):
    return lax.dot_general(a, b, (((1,), (1,)), ((), ())), preferred_element_type=f32)


def dot_tn(a, b):
    return lax.dot_general(a, b, (((0,), (0,)), ((), ())), preferred_element_type=f32)


def in_hbm(a):
    return pltpu.with_memory_space_constraint(a, pltpu.HBM)


def in_vmem(a):
    return pltpu.with_memory_space_constraint(a, pltpu.VMEM)


def whole(shape):
    return pl.BlockSpec(shape, lambda *i: (0,) * len(shape))


SMEM = pl.BlockSpec(memory_space=pltpu.SMEM)
ANY = pl.BlockSpec(memory_space=pl.ANY)
VMEM = pl.BlockSpec(memory_space=pltpu.VMEM)


def sds(shape, dtype):
    return jax.ShapeDtypeStruct(shape, dtype)


def one_minus_exp(z):
    s = 1.0 - z * (1.0 / 8.0)
    for n in (7.0, 6.0, 5.0, 4.0, 3.0, 2.0):
        s = 1.0 - (z * (1.0 / n)) * s
    return z * s


def gelu(v):
    th = jnp.tanh(ROOT * (v + CUBE * v * v * v))
    return 0.5 * v * (1.0 + th)


def gelu_both(v):
    sq = v * v
    th = jnp.tanh(ROOT * v * (1.0 + CUBE * sq))
    half = 0.5 * (1.0 + th)
    slope = half + 0.5 * v * (1.0 - th * th) * (ROOT * (1.0 + 3.0 * CUBE * sq))
    return v * half, slope


class Chain:
    def __init__(self):
        self.token = None

    def __call__(
        self, kernel, args, in_specs, outs, name, grid=(1,), carried=None, scratch=(), mib=32,
        cost=None, loose=(),
    ):
        args, in_specs = list(args), list(in_specs)
        aliases = {}
        for k, a in enumerate(carried or []):
            if a is not None:
                aliases[len(args)] = k
                args.append(a if k in loose else in_hbm(a))
                in_specs.append(ANY)
        n_in = len(args)
        if self.token is not None:
            args.append(self.token)
            in_specs.append(ANY)
        n_all = len(args)
        n_out = len(outs)
        used = n_in - len(aliases)

        def wrapped(*refs):
            refs[n_all + n_out][...] = jnp.zeros((8, 128), f32)
            kernel(*refs[:used], *refs[n_all : n_all + n_out], *refs[n_all + n_out + 1 :])

        *got, self.token = pl.pallas_call(
            wrapped,
            grid=grid,
            in_specs=in_specs,
            out_specs=[out[0] for out in outs] + [whole((8, 128))],
            out_shape=[out[3] if len(out) > 3 else sds(*out[1:3]) for out in outs]
            + [sds((8, 128), f32)],
            scratch_shapes=list(scratch),
            input_output_aliases=aliases,
            compiler_params=pltpu.CompilerParams(
                dimension_semantics=("arbitrary",) * len(grid), vmem_limit_bytes=mib * MIB
            ),
            cost_estimate=cost and pl.CostEstimate(flops=cost, bytes_accessed=1, transcendentals=0),
            name=name,
        )(*args)
        return got


def pinned(spec, shape, dtype):
    return spec, shape, dtype, pltpu.HBM(shape, dtype)


def rows_at(off, tb, width):
    return pl.BlockSpec((pl.Element(tb), pl.Element(width)), lambda *i: (off, 0))


def proj_kernel(x_ref, wy_ref, wx_ref, by_ref, bx_ref, g1_ref, n1_ref, ypre_ref, u_ref):
    n1 = norm(x_ref[...], g1_ref[...])
    n1_ref[...] = n1
    u_ref[...] = (dot(n1, wx_ref[...]) + bx_ref[...]).astype(bf16)
    ypre_ref[...] = dot(n1, wy_ref[...]) + by_ref[...]


def norm(v, gain):
    v = v.astype(f32)
    ms = jnp.mean(v * v, axis=-1, keepdims=True)
    return (v * lax.rsqrt(ms + EPS) * gain).astype(bf16)


def project(chain, x, wy, wx, by, bx, g1, tb):
    rows, width = x.shape
    chan = wy.shape[1]
    spec = lambda w: pl.BlockSpec((tb, w), lambda b: (b, 0))
    return chain(
        proj_kernel, [in_hbm(x), in_hbm(wy), in_hbm(wx), by, bx, g1],
        [spec(width)] + [whole(a.shape) for a in (wy, wx, by, bx, g1)],
        [
            pinned(spec(width), (rows, width), bf16), (spec(chan), (rows, chan), f32),
            (spec(chan), (rows, chan), bf16),
        ],
        "project", grid=(rows // tb,),
    )


def spread_masks(m_ref, kext, keep_row):
    tb = m_ref.shape[0]
    k0 = kext[HALO : HALO + tb, 0:1]
    k1 = kext[HALO - 1 : HALO - 1 + tb, 0:1]
    k2 = kext[HALO - 2 : HALO - 2 + tb, 0:1]
    return k0, k0 * k1, k0 * k1 * k2


def recur_kernel(
    mine_ref, xe_ref, wx_ref, bx_ref, g1_ref, wa_ref, wi_ref, conv_w_ref, conv_b_ref, ba_ref,
    bi_ref, lam_ref, u_ref, flag_ref,
    c_ref, carry_ref, r_ref, i_ref, h_ref, p_ref, end_ref, ue_ref, ke_ref, vec_ref,
    uext, kext, cbuf, dbuf, hs, ps, run,
):
    tb, chan = u_ref.shape
    width = wx_ref.shape[0]
    length = tb // SEGS
    b = pl.program_id(0)

    @pl.when(b == 0)
    def _():
        inside = jnp.where(mine_ref[0] > 0, 1.0, 0.0)
        ne = norm(xe_ref[:, :width], g1_ref[...])
        ue = (dot(ne, wx_ref[...]) + bx_ref[...]).astype(bf16).astype(f32) * inside
        uext[:HALO, :] = ue
        ue_ref[...] = ue
        ke = 1.0 - xe_ref[:, width : width + 128].astype(f32)
        kext[:HALO, :] = ke
        ke_ref[...] = ke
        run[0:1, :] = jnp.ones((1, chan), f32)
        run[1:2, :] = jnp.zeros((1, chan), f32)
        vec_ref[0:4, :] = conv_w_ref[...]
        e = jnp.exp(-lam_ref[...])
        soft = e * (1.0 - e * (0.5 - e * (1.0 / 3.0 - e * (0.25 - e * (0.2 - e * (1.0 / 6.0))))))
        vec_ref[4:5, :] = POWER * soft
        vec_ref[5:6, :] = POWER * e / (1.0 + e)
        vec_ref[6:8, :] = jnp.zeros((2, chan), f32)

    @pl.when(b > 0)
    def _():
        uext[:HALO, :] = uext[tb : tb + HALO, :]
        kext[:HALO, :] = kext[tb : tb + HALO, :]

    uext[HALO:, :] = u_ref[...].astype(f32)
    kext[HALO:, :] = jnp.broadcast_to(1.0 - flag_ref[...].astype(f32), (tb, 128))
    keep, alive2, alive3 = spread_masks(flag_ref, kext, None)
    side = wa_ref.shape[1]
    for k in range(chan // side):
        ln = slice(k * side, (k + 1) * side)
        tap = lambda j: conv_w_ref[j : j + 1, ln]
        conv = conv_b_ref[:, ln] + tap(0) * uext[HALO:, ln]
        conv = conv + tap(1) * uext[HALO - 1 : HALO - 1 + tb, ln] * keep
        conv = conv + tap(2) * uext[HALO - 2 : HALO - 2 + tb, ln] * alive2
        conv = conv + tap(3) * uext[HALO - 3 : HALO - 3 + tb, ln] * alive3
        c = conv.astype(bf16)
        c_ref[:, ln] = c
        r = jax.nn.sigmoid(dot(c, wa_ref[k]) + ba_ref[:, ln])
        i = jax.nn.sigmoid(dot(c, wi_ref[k]) + bi_ref[:, ln])
        r_ref[:, ln] = r
        i_ref[:, ln] = i
        decay = r * vec_ref[4:5, ln]
        mult = (1.0 - keep) + keep * jnp.sqrt(one_minus_exp(2.0 * decay))
        carry = jnp.exp(-decay) * keep
        carry_ref[:, ln] = carry
        cbuf[k] = carry
        dbuf[k] = mult * i * c.astype(f32)
    blocks = chan // 128
    hh = [jnp.zeros((SEGS, 128), f32) for _ in range(blocks)]
    pp = [jnp.ones((SEGS, 128), f32) for _ in range(blocks)]
    for j in range(length):
        rows = pl.ds(j, SEGS, stride=length)
        for k in range(blocks):
            a = cbuf[k, rows, :]
            hh[k] = a * hh[k] + dbuf[k, rows, :]
            pp[k] = a * pp[k]
            hs[k, rows, :] = hh[k]
            ps[k, rows, :] = pp[k]
    for k in range(blocks):
        ln = slice(k * 128, (k + 1) * 128)
        prow = run[0:1, ln]
        hrow = run[1:2, ln]
        for s in range(SEGS):
            rows = slice(s * length, (s + 1) * length)
            pseg = ps[k, rows, :]
            h_ref[rows, ln] = hs[k, rows, :] + pseg * hrow
            p_ref[rows, ln] = pseg * prow
            hrow = hh[k][s : s + 1, :] + pp[k][s : s + 1, :] * hrow
            prow = pp[k][s : s + 1, :] * prow
        run[0:1, ln] = prow
        run[1:2, ln] = hrow
        end_ref[0:1, ln] = prow
        end_ref[1:2, ln] = hrow


def recur(chain, mine, xe, wx, bx, g1, wa, wi, conv_w, conv_b, ba, bi, lam, u, flags, tb):
    rows, chan = u.shape
    spec = lambda w: pl.BlockSpec((tb, w), lambda b: (b, 0))
    fixed = [xe, wx, bx, g1, wa, wi, conv_w, conv_b, ba, bi, lam]
    full = lambda shape: (whole(shape), shape, f32)
    return chain(
        recur_kernel, [mine, *fixed, u, flags],
        [SMEM] + [whole(a.shape) for a in fixed] + [spec(chan), spec(1)],
        [pinned(spec(chan), (rows, chan), bf16)]
        + [pinned(spec(chan), (rows, chan), f32)] * 3
        + [(spec(chan), (rows, chan), f32)] * 2
        + [full((2, chan)), full((HALO, chan)), full((HALO, 128)), full((8, chan))],
        "recur", grid=(rows // tb,),
        scratch=[
            pltpu.VMEM((tb + HALO, chan), f32),
            pltpu.VMEM((tb + HALO, 128), f32),
            *[pltpu.VMEM((chan // 128, tb, 128), f32)] * 4,
            pltpu.VMEM((2, chan), f32),
        ],
    )


def entering(ends_ref, mine, backward):
    count = ends_ref.shape[0]
    total = jnp.zeros_like(ends_ref[0, 1:2, :])
    for s in range(count - 1):
        at = count - 1 - s if backward else s
        new = ends_ref[at, 0:1, :] * total + ends_ref[at, 1:2, :]
        inside = at > mine if backward else at < mine
        total = jnp.where(inside, new, total)
    return total


def out_kernel(mine_ref, ends_ref, wo_ref, h_ref, p_ref, ypre_ref, state_ref, gl_ref, part_ref):
    into = entering(ends_ref, mine_ref[0], False)
    state = h_ref[...] + p_ref[...] * into
    state_ref[...] = state
    gl = (gelu(ypre_ref[...]) * state).astype(bf16)
    gl_ref[...] = gl
    part_ref[...] = dot(gl, wo_ref[...]).astype(bf16)


def by_parts(chain, kernel, chunk, fixed, arrived, chunked, name, **more):
    off, tb = chunk
    step = STEP if off % STEP == 0 and tb % STEP == 0 else tb
    rows, width = chunked[0].shape
    inner = pl.BlockSpec((step, width), lambda i: (i, 0))
    first = off // step
    outer = pl.BlockSpec((step, width), lambda i: (first + i, 0))
    return chain(
        kernel, list(fixed) + list(arrived) + [in_hbm(a) for a in chunked],
        [SMEM if a.dtype == jnp.int32 else whole(a.shape) for a in fixed]
        + [inner] * len(arrived) + [outer] * len(chunked),
        [pinned(outer, (rows, width), bf16)], name, grid=(tb // step,), **more,
    )


def chunk_call(chain, kernel, chunk, fixed, chunked, outs, own, name, free=False, held=(), **more):
    off, tb = chunk
    rows = chunked[0].shape[0]
    ins = [SMEM if a.dtype == jnp.int32 else whole(a.shape) for a in fixed]
    ins += [VMEM] * len(held)
    return chain(
        kernel, list(fixed) + [in_vmem(a) for a in held] + [a if free else in_hbm(a) for a in chunked],
        ins + [rows_at(off, tb, a.shape[1]) for a in chunked],
        [pinned(rows_at(off, tb, w), (rows, w), d) for w, d in outs]
        + [(whole(s), s, d) for s, d in own],
        name, **more,
    )


def out_chunk(chain, chunk, mine, h, p, ypre, ends, wo, carried):
    chan, width = wo.shape
    return chunk_call(
        chain, out_kernel, chunk, [mine, ends, wo], [h, p, ypre], [(chan, f32), (chan, bf16)],
        [((chunk[1], width), bf16)], "out_proj", carried=carried, free=True,
    )


def slopes_kernel(
    mine_ref, ends_ref, vec_ref, r_ref, i_ref, carry_ref, c_ref, state_ref, before_ref, flag_ref,
    *rest,
):
    a_ref, b_ref, d_ref, g_ref, sext = rest[-5:]
    tb = r_ref.shape[0]
    b = pl.program_id(0)
    sext[8:, :] = state_ref[...]
    sext[:8, :] = before_ref[...]

    @pl.when(b == 0)
    def _():
        sext[7:8, :] = entering(ends_ref, mine_ref[0], False)

    keep = 1.0 - flag_ref[...].astype(f32)
    sp = vec_ref[4:5, :]
    r = r_ref[...]
    i = i_ref[...]
    c = c_ref[...].astype(f32)
    m2 = one_minus_exp(2.0 * (r * sp))
    m = jnp.sqrt(m2)
    mult = (1.0 - keep) + keep * m
    prior = sext[7 : 7 + tb, :]
    grad = prior * carry_ref[...] - i * c * keep * (1.0 - m2) / m
    gr = grad * r
    g_ref[...] = gr
    a_ref[...] = -gr * sp * (1.0 - r)
    mi = mult * i
    b_ref[...] = mi * c * (1.0 - i)
    d_ref[...] = mi


def slopes(chain, mine, ends, vec, r, i, carry, c, state, flags, tb, ahead):
    rows, chan = r.shape
    spec = lambda w: pl.BlockSpec((tb, w), lambda b: (b, 0))
    before = pl.BlockSpec((8, chan), lambda b: (jnp.maximum(b * (tb // 8) - 1, 0), 0))
    return chain(
        slopes_kernel,
        [mine, ends, vec] + [in_hbm(a) for a in (r, i, carry, c, state, state)] + [flags]
        + [in_vmem(a) for a in ahead],
        [SMEM, whole(ends.shape), whole(vec.shape)] + [spec(chan)] * 5 + [before, spec(1)]
        + [VMEM] * len(ahead),
        [pinned(spec(chan), (rows, chan), f32)] * 4,
        "slopes", grid=(rows // tb,), scratch=[pltpu.VMEM((tb + 8, chan), f32)],
    )


def pick(mid_ref, t_ref, far_ref):
    mid = mid_ref[0] == 1
    return jnp.where(mid, t_ref[...], far_ref[...])


def mlp_kernel(
    mid_ref, g2_ref, t_ref, far_ref, wg_ref, wu_ref, wd_ref, x_ref, cot_ref,
    rec_ref, n2_ref, hid_ref, dg_ref, du_ref, mpart_ref, dpart_ref,
):
    rec = pick(mid_ref, t_ref, far_ref)
    rec_ref[...] = rec
    n2 = norm(x_ref[...].astype(f32) + rec.astype(f32), g2_ref[...])
    n2_ref[...] = n2
    gpre = dot(n2, wg_ref[...])
    up = dot(n2, wu_ref[...])
    dh = dot_nt(cot_ref[...], wd_ref[...])
    act, slope = gelu_both(gpre)
    hid = (act * up).astype(bf16)
    dg = (dh * up * slope).astype(bf16)
    du = (dh * act).astype(bf16)
    hid_ref[...] = hid
    dg_ref[...] = dg
    du_ref[...] = du
    dpart_ref[...] = (dot_nt(dg, wg_ref[...]) + dot_nt(du, wu_ref[...])).astype(bf16)
    mpart_ref[...] = dot(hid, wd_ref[...]).astype(bf16)


def mlp_chunk(chain, chunk, group, mid, t, far, g2, wg, wu, wd, x, cot, carried, mpart):
    rows, width = x.shape
    hidden = wg.shape[1]
    off, tb = chunk
    base, size = group
    put = lambda w, d=bf16: pinned(rows_at(off, tb, w), (rows, w), d)
    return chain(
        mlp_kernel, [mid, g2, t, far, *[in_vmem(a) for a in (wg, wu, wd)], in_hbm(x), in_hbm(cot)],
        [SMEM, whole(g2.shape), whole(t.shape), whole(far.shape), VMEM, VMEM, VMEM]
        + [rows_at(off, tb, width)] * 2,
        [put(width), put(width), put(hidden), put(hidden), put(hidden)]
        + [(rows_at(off - base, tb, width), (size, width), bf16)]
        + [(whole((tb, width)), (tb, width), bf16)],
        "mlp", carried=(carried or [None] * 5) + [mpart], loose=(5,), mib=36,
    )


def back_kernel(
    mid_ref, t_ref, far_ref, g2_ref, wo_ref, run_ref,
    x_ref, rec_ref, cot_ref, state_ref, ypre_ref, carry_ref,
    drec_ref, branch_ref, adj_ref, q_ref, end_ref, dg2_ref, cbuf, dbuf, al, ql,
):
    tb = x_ref.shape[0]
    chan = wo_ref.shape[0]
    length = tb // SEGS
    dn = pick(mid_ref, t_ref, far_ref).astype(f32)
    x2 = x_ref[...].astype(f32) + rec_ref[...].astype(f32)
    inv = lax.rsqrt(jnp.mean(x2 * x2, axis=-1, keepdims=True) + EPS)
    hat = x2 * inv
    dh = dn * hat
    dg2_ref[...] = jnp.sum(dh, axis=0, keepdims=True)
    g2 = g2_ref[...]
    dot_mean = jnp.mean(dh * g2, axis=-1, keepdims=True)
    dx2 = cot_ref[...].astype(f32) + inv * (dn * g2 - hat * dot_mean)
    drec = dx2.astype(bf16)
    drec_ref[...] = drec
    dgl = dot_nt(drec, wo_ref[...])
    y, slope = gelu_both(ypre_ref[...])
    branch_ref[...] = (dgl * state_ref[...] * slope).astype(bf16)
    dstate = dgl * y
    blocks = chan // 128
    for k in range(blocks):
        ln = slice(k * 128, (k + 1) * 128)
        cbuf[k] = carry_ref[:, ln]
        dbuf[k] = dstate[:, ln]
    ee = [jnp.zeros((SEGS, 128), f32) for _ in range(blocks)]
    qq = [jnp.ones((SEGS, 128), f32) for _ in range(blocks)]
    for j in range(length - 1, -1, -1):
        rows = pl.ds(j, SEGS, stride=length)
        for k in range(blocks):
            a = cbuf[k, rows, :]
            adj = dbuf[k, rows, :] + ee[k]
            al[k, rows, :] = adj
            ql[k, rows, :] = qq[k]
            ee[k] = a * adj
            qq[k] = a * qq[k]
    for k in range(blocks):
        ln = slice(k * 128, (k + 1) * 128)
        qrow = run_ref[0:1, ln]
        erow = run_ref[1:2, ln]
        for s in range(SEGS - 1, -1, -1):
            rows = slice(s * length, (s + 1) * length)
            qseg = ql[k, rows, :]
            adj_ref[rows, ln] = al[k, rows, :] + qseg * erow
            q_ref[rows, ln] = qseg * qrow
            qend = qq[k][s : s + 1, :]
            erow = ee[k][s : s + 1, :] + qend * erow
            qrow = qend * qrow
        end_ref[0:1, ln] = qrow
        end_ref[1:2, ln] = erow


def back_chunk(chain, chunk, mid, t, far, g2, wo, run, x, rec, cot, state, ypre, carry, carried):
    chan, width = wo.shape
    return chunk_call(
        chain, back_kernel, chunk, [mid, t, far, g2, wo, run], [x, rec, cot, state, ypre, carry],
        [(width, bf16), (chan, bf16), (chan, f32), (chan, f32)],
        [((2, chan), f32), ((1, width), f32)], "mid_back", carried=carried,
        scratch=[pltpu.VMEM((chan // 128, chunk[1], 128), f32)] * 4,
    )


def gates_kernel(
    mine_ref, ends_ref, vec_ref, wa_ref, wi_ref, ue_ref, ke_ref,
    adj_ref, q_ref, a_ref, b_ref, d_ref, g_ref, c_ref, u_ref, before_ref, flag_ref, flag_before_ref,
    branch_ref, du_ref, tail_ref, edge_ref, gwa_ref, gwi_ref, sums_ref, uext, kext, e1, e2, e3,
):
    tb, chan = adj_ref.shape
    step = pl.program_id(0)
    steps = pl.num_programs(0)
    side = wa_ref.shape[1]
    vec = lambda k: vec_ref[k : k + 1, :]

    @pl.when(step == 0)
    def _():
        for e in (e1, e2, e3):
            e[tb:, :] = jnp.zeros((8, chan), f32)
        gwa_ref[...] = jnp.zeros_like(gwa_ref)
        gwi_ref[...] = jnp.zeros_like(gwi_ref)
        sums_ref[...] = jnp.zeros_like(sums_ref)

    @pl.when(step > 0)
    def _():
        for e in (e1, e2, e3):
            e[tb:, :] = e[:8, :]

    uext[HALO:, :] = u_ref[...].astype(f32)
    kext[HALO:, :] = jnp.broadcast_to(1.0 - flag_ref[...].astype(f32), (tb, 128))

    @pl.when(step == steps - 1)
    def _():
        uext[:HALO, :] = ue_ref[...]
        kext[:HALO, :] = ke_ref[...]

    @pl.when(step < steps - 1)
    def _():
        uext[:HALO, :] = before_ref[...].astype(f32)
        kext[:HALO, :] = jnp.broadcast_to(1.0 - flag_before_ref[...].astype(f32), (HALO, 128))

    into = entering(ends_ref, mine_ref[0], True)
    keep, alive2, alive3 = spread_masks(flag_ref, kext, None)

    def add(k, ln, value):
        sums_ref[k : k + 1, ln] += jnp.sum(value, axis=0, keepdims=True)

    for k in range(chan // side):
        ln = slice(k * side, (k + 1) * side)
        adj = adj_ref[:, ln] + q_ref[:, ln] * into[:, ln]
        add(2, ln, adj * g_ref[:, ln])
        da = (adj * a_ref[:, ln]).astype(bf16)
        di = (adj * b_ref[:, ln]).astype(bf16)
        add(0, ln, da.astype(f32))
        add(1, ln, di.astype(f32))
        gwa_ref[k] += dot_tn(c_ref[:, ln], da)
        gwi_ref[k] += dot_tn(c_ref[:, ln], di)
        dconv = adj * d_ref[:, ln] + dot_nt(da, wa_ref[k]) + dot_nt(di, wi_ref[k])
        add(3, ln, dconv)
        add(4, ln, dconv * uext[HALO:, ln])
        mk = dconv * keep
        e1[:tb, ln] = mk
        add(5, ln, mk * uext[HALO - 1 : HALO - 1 + tb, ln])
        mk = dconv * alive2
        e2[:tb, ln] = mk
        add(6, ln, mk * uext[HALO - 2 : HALO - 2 + tb, ln])
        mk = dconv * alive3
        e3[:tb, ln] = mk
        add(7, ln, mk * uext[HALO - 3 : HALO - 3 + tb, ln])
        v = lambda j: vec_ref[j : j + 1, ln]
        du = v(0) * dconv + v(1) * e1[1 : 1 + tb, ln]
        du = du + v(2) * e2[2 : 2 + tb, ln] + v(3) * e3[3 : 3 + tb, ln]
        low = du.astype(bf16)
        du_ref[:, ln] = low
        add(8, ln, low.astype(f32))
        add(9, ln, branch_ref[:, ln].astype(f32))

        @pl.when(step == 0)
        def _():
            tail_ref[:, ln] = du[tb - HALO :, :]
            sums_ref[8:9, ln] -= jnp.sum(low[tb - HALO :, :].astype(f32), axis=0, keepdims=True)

    @pl.when(step == steps - 1)
    def _():
        edge_ref[...] = jnp.zeros_like(edge_ref)
        edge_ref[5:6, :] = vec(3) * e3[0:1, :]
        edge_ref[6:7, :] = vec(2) * e2[0:1, :] + vec(3) * e3[1:2, :]
        edge_ref[7:8, :] = vec(1) * e1[0:1, :] + vec(2) * e2[1:2, :] + vec(3) * e3[2:3, :]
        sums_ref[2:3, :] = sums_ref[2:3, :] * vec(5)


def gates_back(chain, mine, ends, vec, wa, wi, ue, ke, adj, q, slope4, c, u, flags, branch, tb):
    rows, chan = adj.shape
    n = rows // tb
    spec = lambda w: pl.BlockSpec((tb, w), lambda b: (n - 1 - b, 0))
    per = tb // HALO
    before = lambda w: pl.BlockSpec((HALO, w), lambda b: (jnp.maximum((n - 1 - b) * per - 1, 0), 0))
    full = lambda shape: (whole(shape), shape, f32)
    fixed = [ends, vec, wa, wi, ue, ke]
    return chain(
        gates_kernel,
        [mine, *fixed] + [in_hbm(a) for a in (adj, q, *slope4, c, u, u)] + [flags, flags]
        + [in_hbm(branch)],
        [SMEM] + [whole(a.shape) for a in fixed] + [spec(chan)] * 8
        + [before(chan), spec(1), before(1), spec(chan)],
        [
            pinned(spec(chan), (rows, chan), bf16), full((HALO, chan)), full((8, chan)), full(wa.shape),
            full(wi.shape), full((16, chan)),
        ],
        "gates_back", grid=(n,), mib=40, cost=LONG_G,
        scratch=[pltpu.VMEM((tb + HALO, chan), f32), pltpu.VMEM((tb + HALO, 128), f32)]
        + [pltpu.VMEM((tb + 8, chan), f32)] * 3,
    )


def in_kernel(wy_ref, wx_ref, x_ref, branch_ref, du_ref, part_ref, dg1_ref):
    part = dot_nt(branch_ref[...], wy_ref[...]) + dot_nt(du_ref[...], wx_ref[...])
    part_ref[...] = part.astype(bf16)
    x = x_ref[...].astype(f32)
    inv = lax.rsqrt(jnp.mean(x * x, axis=-1, keepdims=True) + EPS)
    dg1_ref[...] = jnp.sum(part * (x * inv), axis=0, keepdims=True)


def in_chunk(chain, chunk, wy, wx, x, branch, du):
    width = x.shape[1]
    return chunk_call(
        chain, in_kernel, chunk, [wy, wx], [x, branch, du], [],
        [((chunk[1], width), bf16), ((1, width), f32)], "in_back",
    )


def result_kernel(mid_ref, t_ref, far_ref, x_ref, rec_ref, out_ref):
    total = x_ref[...].astype(f32) + rec_ref[...].astype(f32)
    out_ref[...] = (total + pick(mid_ref, t_ref, far_ref).astype(f32)).astype(bf16)


def result_chunk(chain, chunk, mid, t, far, x, rec, carried):
    return by_parts(
        chain, result_kernel, chunk, [mid], [t, far], [x, rec], "result", carried=carried
    )


def last_kernel(mid_ref, g1_ref, t_ref, far_ref, x_ref, dx2_ref, out_ref):
    dn = pick(mid_ref, t_ref, far_ref).astype(f32) * g1_ref[...]
    x = x_ref[...].astype(f32)
    inv = lax.rsqrt(jnp.mean(x * x, axis=-1, keepdims=True) + EPS)
    hat = x * inv
    mean = jnp.mean(dn * hat, axis=-1, keepdims=True)
    out_ref[...] = (dx2_ref[...].astype(f32) + inv * (dn - hat * mean)).astype(bf16)


def last_chunk(chain, chunk, mid, t, far, g1, x, dx2, carried, cost):
    return by_parts(
        chain, last_kernel, chunk, [mid, g1], [t, far], [x, dx2], "stream_grad", carried=carried,
        cost=cost,
    )


def weight_grad(chain, a, b, at, columns, db, carried):
    height, wide = a.shape[1], b.shape[1]

    def kernel(a_ref, b_ref, out_ref):
        out_ref[...] = dot_tn(a_ref[...], b_ref[...]).astype(bf16)

    rows = a.shape[0]
    return chain(
        kernel, [in_hbm(a), in_hbm(b)],
        [pl.BlockSpec((rows, db), lambda i: (0, i)), whole(b.shape)],
        [pinned(pl.BlockSpec((db, wide), lambda i: (i, at)), (height, columns), bf16)],
        "weight_grad", grid=(height // db,), carried=carried, mib=24,
    )


def widen(chain, total, name):
    rows, columns = total.shape
    third = columns // 3

    def kernel(t_ref, a_ref, b_ref, c_ref):
        a_ref[...] = t_ref[:, :third].astype(f32)
        b_ref[...] = t_ref[:, third : 2 * third].astype(f32)
        c_ref[...] = t_ref[:, 2 * third :].astype(f32).T

    shapes = [(rows, third), (rows, third), (third, rows)]
    return chain(
        kernel, [total], [whole(total.shape)], [(whole(s), s, f32) for s in shapes], name
    )


def add_pair(chain, a, b):
    def kernel(a_ref, b_ref, out_ref):
        out_ref[...] = (a_ref[...].astype(f32) + b_ref[...].astype(f32)).astype(out_ref.dtype)

    return chain(
        kernel, [a, b], [whole(a.shape), whole(b.shape)], [(whole(a.shape), a.shape, a.dtype)],
        "hop_sum",
    )[0]


class Fold:
    def __init__(self, chain, axis):
        self.chain = chain
        self.axis = axis
        self.line = lax.axis_size(axis) == 4

    def start(self, part):
        self.part = part
        if self.line:
            self.got = lax.ppermute(part, self.axis, [(0, 1), (3, 2)])
        else:
            self.t = self.far = lax.psum(part, self.axis)

    def swap(self):
        if self.line:
            self.part = add_pair(self.chain, self.part, self.got)
            self.got = lax.ppermute(self.part, self.axis, [(1, 2), (2, 1)])

    def back(self):
        if self.line:
            self.t = add_pair(self.chain, self.part, self.got)
            self.far = lax.ppermute(self.t, self.axis, [(1, 0), (2, 3)])

    def pair(self):
        return self.t, self.far


class Exchange:
    def __init__(self, chain, value, axis):
        self.chain, self.axis, self.value = chain, axis, value
        self.n = lax.axis_size(axis)
        self.bit = 1
        if self.n & (self.n - 1):
            self.value = lax.psum(value, axis)
            self.bit = self.n
        self.send()

    def send(self):
        if self.bit < self.n:
            route = [(i, i ^ self.bit) for i in range(self.n)]
            self.got = lax.ppermute(self.value, self.axis, route)

    def step(self):
        if self.bit < self.n:
            self.value = add_pair(self.chain, self.value, self.got)
            self.bit *= 2
            self.send()

    def finish(self):
        while self.bit < self.n:
            self.step()
        return self.value


def split(sizes):
    chunks, off = [], 0
    for size in sizes:
        chunks.append((off, size))
        off += size
    return chunks


def body(
    x, prescale, wy, by, wx, bx, conv_w, conv_b, wa, ba, wi, bi, lam, wo, midscale, wg, wu, wd,
    resets, cot,
):
    rows, width = x.shape
    chan = wy.shape[1]
    hidden = wg.shape[1]
    blocks, side = wa.shape[:2]
    n_seq = lax.axis_size("seq")
    n_head = lax.axis_size("head")
    mine = lax.axis_index("seq").astype(jnp.int32)[None]
    me = lax.axis_index("head")
    mid = ((me == 1) | (me == 2)).astype(jnp.int32)[None]
    chain = Chain()
    tb = 256
    sizes = FIRST if sum(FIRST) == rows else [rows // 4] * 4
    one = split(sizes)[::-1]
    sizes = LAST if sum(LAST) == rows else [rows // 4] * 4
    two = split(sizes)

    g1, g2 = prescale[None], midscale[None]
    flags = resets[:, None]
    packed = jnp.concatenate(
        [x[rows - HALO :], jnp.broadcast_to(flags[rows - HALO :], (HALO, 128)).astype(bf16)], axis=1
    )
    forward = [(i, i + 1) for i in range(n_seq - 1)]
    backward = [(i + 1, i) for i in range(n_seq - 1)]
    xe = lax.ppermute(packed, "seq", forward)
    n1, ypre, u = project(chain, x, wy, wx, by[None], bx[None], g1, tb)
    c, carry, r, i, h, p, end, ue, ke, vec = recur(
        chain, mine, xe, wx, bx[None], g1, wa, wi, conv_w, conv_b[None], ba[None], bi[None],
        lam[None], u, flags, tb,
    )
    ends = lax.all_gather(end, "seq")

    n = len(one)
    rec_f = [Fold(chain, "head") for _ in one]
    n2_f = [Fold(chain, "head") for _ in one]
    n1_f = [Fold(chain, "head") for _ in two]
    groups = one
    mlp_f = [Fold(chain, "head") for _ in groups]
    d = {}

    kept = None
    for k in range(n):
        *kept, part = out_chunk(chain, one[k], mine, h, p, ypre, ends, wo, kept)
        rec_f[k].start(part)
    state, gl = kept
    slope4 = slopes(
        chain, mine, ends, vec, r, i, carry, c, state, flags, tb, (wg, wu, wd)
    )

    def mlp(k):
        g = k * len(groups) // n
        *d["mlp"], d["mp", g], dp = mlp_chunk(
            chain, one[k], groups[g], mid, *rec_f[k].pair(), g2, wg, wu, wd, x, cot, d.get("mlp"),
            d.get(("mp", g)),
        )
        n2_f[k].start(dp)

    def back(k):
        run = d.get("run")
        if run is None:
            run = jnp.concatenate([jnp.ones((1, chan), f32), jnp.zeros((1, chan), f32)])
        *d["back"], d["run"], dg2 = back_chunk(
            chain, one[k], mid, *n2_f[k].pair(), g2, wo, run, x, d["mlp"][0], cot, state, ypre,
            carry, d.get("back"),
        )
        d["g2"] = d.get("g2", 0.0) + dg2

    def big(k):
        rec, n2, hid, dg, du2 = d["mlp"]
        a, b = ((n2, dg), (n2, du2), (cot, hid))[k]
        d["big"] = weight_grad(chain, a, b, k, 3 * hidden, 512, d.get("big"))

    def start_mlp(k):
        mlp_f[k].start(d["mp", k])

    def result(k):
        d["result"] = result_chunk(
            chain, groups[k], mid, *mlp_f[k].pair(), x, d["mlp"][0], d.get("result")
        )

    def scatter():
        d["big_sum"] = lax.psum_scatter(d["big"][0], "seq", scatter_dimension=0, tiled=True)

    def gather():
        d["ends"] = lax.all_gather(d["run"], "seq")

    def gates():
        drec, branch, adj, q = d["back"]
        d["du"], d["tail"], edge, d["gwa"], d["gwi"], d["sums"] = gates_back(
            chain, mine, d["ends"], vec, wa, wi, ue, ke, adj, q, slope4, c, u, flags, branch, tb
        )
        d["edge"] = lax.ppermute(edge, "seq", backward)

    def patched():
        patch = d["tail"] + jnp.concatenate([jnp.zeros((HALO - 8, chan), f32), d["edge"]])
        patch = patch.astype(bf16)
        d["du"] = lax.dynamic_update_slice(d["du"], patch, (rows - HALO, 0))
        d["sums"] = d["sums"].at[8].add(jnp.sum(patch.astype(f32), axis=0))

    def inner(k):
        part, dg1 = in_chunk(chain, two[k], wy, wx, x, d["back"][1], d["du"])
        d["g1"] = d.get("g1", 0.0) + dg1
        n1_f[k].start(part)

    def lru_weights(k):
        drec, branch, adj, q = d["back"]
        a, b = ((n1, branch), (n1, d["du"]), (drec, gl))[k]
        d["small"] = weight_grad(chain, a, b, k, 3 * chan, 512, d.get("small"))

    def scatter_small():
        d["small_sum"] = lax.psum_scatter(d["small"][0], "seq", scatter_dimension=0, tiled=True)

    def stacked():
        gains = jnp.concatenate([d["g1"], d["g2"] * (1.0 / n_head)])
        pieces = [d[name].reshape(-1, side) for name in ("gwa", "gwi", "sums")]
        pieces.append(gains.reshape(-1, side))
        cuts = [0]
        for piece in pieces:
            cuts.append(cuts[-1] + piece.shape[0])
        d["cuts"] = cuts
        stack = jnp.concatenate(pieces + [jnp.zeros((-cuts[-1] % 16, side), f32)]).astype(bf16)
        d["stack"] = Exchange(chain, stack, "seq")

    def stack_step():
        d["stack"].step()

    def head_start():
        d["total"] = d["stack"].finish()
        d["gains"] = Exchange(chain, d["total"][d["cuts"][3] :], "head")

    def head_step():
        d["gains"].step()

    def widen_big():
        d["big_out"] = widen(chain, d["big_sum"], "mlp_grads")

    def widen_small():
        d["small_out"] = widen(chain, d["small_sum"], "lru_grads")

    def last(k):
        d["last"] = last_chunk(
            chain, two[k], mid, *n1_f[k].pair(), g1, x, d["back"][0], d.get("last"),
            LONG if k == len(two) - 1 else None,
        )

    calls = {
        "Rs": lambda k: rec_f[k].swap(), "Rb": lambda k: rec_f[k].back(), "M": mlp,
        "Ns": lambda k: n2_f[k].swap(), "Nb": lambda k: n2_f[k].back(), "B": back, "W": big,
        "I": inner, "X": patched, "V": lru_weights, "As": lambda k: n1_f[k].swap(),
        "Ab": lambda k: n1_f[k].back(), "L": last, "P": start_mlp, "T": result,
        "Ps": lambda k: mlp_f[k].swap(), "Pb": lambda k: mlp_f[k].back(), "scatter": scatter,
        "gather": gather, "gates": gates, "scatter_small": scatter_small, "stack": stacked,
        "stack_step": stack_step, "head": head_start, "head_step": head_step, "big": widen_big,
        "small": widen_small,
    }
    for line in ORDER:
        for step in line.split():
            name = step.rstrip("0123456789")
            calls[name](*([int(step[len(name) :])] if step != name else []))

    g_y, g_x, g_o = d["small_out"]
    g_gate, g_up, g_down = d["big_out"]
    cuts = d["cuts"]
    total = d["total"].astype(f32)
    gains = d["gains"].finish()[: cuts[4] - cuts[3]].astype(f32).reshape(2, width)
    gwa = total[: cuts[1]].reshape(wa.shape)
    gwi = total[cuts[1] : cuts[2]].reshape(wi.shape)
    sums = total[cuts[2] : cuts[3]].reshape(16, chan)
    piece = width // n_seq
    gains = lax.dynamic_slice(gains, (0, mine[0] * piece), (2, piece))
    return (
        d["result"][0], d["last"][0], gains[0], g_y, sums[9], g_x, sums[8], sums[4:8], sums[3],
        gwa, sums[0], gwi, sums[1], sums[2], g_o, gains[1], g_gate, g_up, g_down,
    )


LONG = 3 * 10**10
LONG_G = 10**13
STEP = 128
FIRST = [256, 256, 256, 256]
LAST = [256, 256, 256, 256]

ORDER = [
    "Rs0 Rs1 Rb0 Rs2", "Rb1 M0 P0 Rs3", "Rb2 M1 P1 Ns0", "Rb3 M2 P2 Ns1", "Nb0 M3 P3 Ns2",
    "Nb1 W0 B0 W1", "Ns3 Ps0 Nb2 W2", "scatter B1 Nb3 Ps1", "Pb0 B2 Ps2 Pb1",
    "B3 gather gates Ps3", "Pb2 T0 I0 I1", "I2 T1 X I3", "Pb3 T2 As0 V0", "V2 stack As1 Ab0",
    "T3 V1 scatter_small stack_step", "As2 Ab1 L0 stack_step", "As3 Ab2 L1 stack_step",
    "head Ab3 L2 head_step", "head_step L3 big small",
]


def solution(mesh):
    col, row, both = P(None, "head"), P("head", None), P("seq", "head")
    head, seq, cube = P("head"), P("seq"), P("head", None, None)
    tokens = P("seq", None)
    in_specs = (
        tokens, P(), col, head, col, head, col, head, cube, head, cube, head, head, row, P(), col,
        col, row, seq, tokens,
    )
    out_specs = (
        tokens, tokens, seq, both, head, both, head, col, head, cube, head, cube, head, head,
        P("head", "seq"), seq, both, both, P("head", "seq"),
    )
    return jax.shard_map(body, mesh=mesh, in_specs=in_specs, out_specs=out_specs, check_vma=False)
```

```python
import functools
import jax
import jax.numpy as jnp
from jax import lax
from jax.experimental import pallas as pl
from jax.experimental.pallas import tpu as pltpu
from jax.sharding import PartitionSpec as P

f32 = jnp.float32
bf16 = jnp.bfloat16
EPS = 1e-06
POWER = 8.0
HALO = 16
SEGS = 8
MIB = 1 << 20
ROOT = 0.7978845608028654
CUBE = 0.044715


def dot(a, b):
    return jnp.dot(a, b, preferred_element_type=f32)


def dot_nt(a, b):
    return lax.dot_general(a, b, (((1,), (1,)), ((), ())), preferred_element_type=f32)


def dot_tn(a, b):
    return lax.dot_general(a, b, (((0,), (0,)), ((), ())), preferred_element_type=f32)


def in_hbm(a):
    return pltpu.with_memory_space_constraint(a, pltpu.HBM)


def in_vmem(a):
    return pltpu.with_memory_space_constraint(a, pltpu.VMEM)


def whole(shape):
    return pl.BlockSpec(shape, lambda *i: (0,) * len(shape))


SMEM = pl.BlockSpec(memory_space=pltpu.SMEM)
ANY = pl.BlockSpec(memory_space=pl.ANY)
VMEM = pl.BlockSpec(memory_space=pltpu.VMEM)


def sds(shape, dtype):
    return jax.ShapeDtypeStruct(shape, dtype)


def one_minus_exp(z):
    s = 1.0 - z * (1.0 / 8.0)
    for n in (7.0, 6.0, 5.0, 4.0, 3.0, 2.0):
        s = 1.0 - (z * (1.0 / n)) * s
    return z * s


def gelu(v):
    th = jnp.tanh(ROOT * (v + CUBE * v * v * v))
    return 0.5 * v * (1.0 + th)


def gelu_both(v):
    sq = v * v
    th = jnp.tanh(ROOT * v * (1.0 + CUBE * sq))
    half = 0.5 * (1.0 + th)
    slope = half + 0.5 * v * (1.0 - th * th) * (ROOT * (1.0 + 3.0 * CUBE * sq))
    return v * half, slope


class Chain:
    def __init__(self):
        self.token = None

    def __call__(
        self, kernel, args, in_specs, outs, name, grid=(1,), carried=None, scratch=(), mib=32,
        cost=None, loose=(),
    ):
        args, in_specs = list(args), list(in_specs)
        aliases = {}
        for k, a in enumerate(carried or []):
            if a is not None:
                aliases[len(args)] = k
                args.append(a if k in loose else in_hbm(a))
                in_specs.append(ANY)
        n_in = len(args)
        if self.token is not None:
            args.append(self.token)
            in_specs.append(ANY)
        n_all = len(args)
        n_out = len(outs)
        used = n_in - len(aliases)

        def wrapped(*refs):
            refs[n_all + n_out][...] = jnp.zeros((8, 128), f32)
            kernel(*refs[:used], *refs[n_all : n_all + n_out], *refs[n_all + n_out + 1 :])

        *got, self.token = pl.pallas_call(
            wrapped,
            grid=grid,
            in_specs=in_specs,
            out_specs=[out[0] for out in outs] + [whole((8, 128))],
            out_shape=[out[3] if len(out) > 3 else sds(*out[1:3]) for out in outs]
            + [sds((8, 128), f32)],
            scratch_shapes=list(scratch),
            input_output_aliases=aliases,
            compiler_params=pltpu.CompilerParams(
                dimension_semantics=("arbitrary",) * len(grid), vmem_limit_bytes=mib * MIB
            ),
            cost_estimate=cost and pl.CostEstimate(flops=cost, bytes_accessed=1, transcendentals=0),
            name=name,
        )(*args)
        return got


def pinned(spec, shape, dtype):
    return spec, shape, dtype, pltpu.HBM(shape, dtype)


def rows_at(off, tb, width):
    return pl.BlockSpec((pl.Element(tb), pl.Element(width)), lambda *i: (off, 0))


def proj_kernel(x_ref, wy_ref, wx_ref, by_ref, bx_ref, g1_ref, n1_ref, ypre_ref, u_ref):
    n1 = norm(x_ref[...], g1_ref[...])
    n1_ref[...] = n1
    u_ref[...] = (dot(n1, wx_ref[...]) + bx_ref[...]).astype(bf16)
    ypre_ref[...] = dot(n1, wy_ref[...]) + by_ref[...]


def norm(v, gain):
    v = v.astype(f32)
    ms = jnp.mean(v * v, axis=-1, keepdims=True)
    return (v * lax.rsqrt(ms + EPS) * gain).astype(bf16)


def project(chain, x, wy, wx, by, bx, g1, tb):
    rows, width = x.shape
    chan = wy.shape[1]
    spec = lambda w: pl.BlockSpec((tb, w), lambda b: (b, 0))
    return chain(
        proj_kernel, [in_hbm(x), in_hbm(wy), in_hbm(wx), by, bx, g1],
        [spec(width)] + [whole(a.shape) for a in (wy, wx, by, bx, g1)],
        [
            pinned(spec(width), (rows, width), bf16), (spec(chan), (rows, chan), f32),
            (spec(chan), (rows, chan), bf16),
        ],
        "project", grid=(rows // tb,),
    )


def spread_masks(m_ref, kext, keep_row):
    tb = m_ref.shape[0]
    k0 = kext[HALO : HALO + tb, 0:1]
    k1 = kext[HALO - 1 : HALO - 1 + tb, 0:1]
    k2 = kext[HALO - 2 : HALO - 2 + tb, 0:1]
    return k0, k0 * k1, k0 * k1 * k2


def recur_kernel(
    mine_ref, xe_ref, wx_ref, bx_ref, g1_ref, wa_ref, wi_ref, conv_w_ref, conv_b_ref, ba_ref,
    bi_ref, lam_ref, u_ref, flag_ref,
    c_ref, carry_ref, r_ref, i_ref, h_ref, p_ref, end_ref, ue_ref, ke_ref, vec_ref,
    uext, kext, cbuf, dbuf, hs, ps, run,
):
    tb, chan = u_ref.shape
    width = wx_ref.shape[0]
    length = tb // SEGS
    b = pl.program_id(0)

    @pl.when(b == 0)
    def _():
        inside = jnp.where(mine_ref[0] > 0, 1.0, 0.0)
        ne = norm(xe_ref[:, :width], g1_ref[...])
        ue = (dot(ne, wx_ref[...]) + bx_ref[...]).astype(bf16).astype(f32) * inside
        uext[:HALO, :] = ue
        ue_ref[...] = ue
        ke = 1.0 - xe_ref[:, width : width + 128].astype(f32)
        kext[:HALO, :] = ke
        ke_ref[...] = ke
        run[0:1, :] = jnp.ones((1, chan), f32)
        run[1:2, :] = jnp.zeros((1, chan), f32)
        vec_ref[0:4, :] = conv_w_ref[...]
        e = jnp.exp(-lam_ref[...])
        soft = e * (1.0 - e * (0.5 - e * (1.0 / 3.0 - e * (0.25 - e * (0.2 - e * (1.0 / 6.0))))))
        vec_ref[4:5, :] = POWER * soft
        vec_ref[5:6, :] = POWER * e / (1.0 + e)
        vec_ref[6:8, :] = jnp.zeros((2, chan), f32)

    @pl.when(b > 0)
    def _():
        uext[:HALO, :] = uext[tb : tb + HALO, :]
        kext[:HALO, :] = kext[tb : tb + HALO, :]

    uext[HALO:, :] = u_ref[...].astype(f32)
    kext[HALO:, :] = jnp.broadcast_to(1.0 - flag_ref[...].astype(f32), (tb, 128))
    keep, alive2, alive3 = spread_masks(flag_ref, kext, None)
    side = wa_ref.shape[1]
    for k in range(chan // side):
        ln = slice(k * side, (k + 1) * side)
        tap = lambda j: conv_w_ref[j : j + 1, ln]
        conv = conv_b_ref[:, ln] + tap(0) * uext[HALO:, ln]
        conv = conv + tap(1) * uext[HALO - 1 : HALO - 1 + tb, ln] * keep
        conv = conv + tap(2) * uext[HALO - 2 : HALO - 2 + tb, ln] * alive2
        conv = conv + tap(3) * uext[HALO - 3 : HALO - 3 + tb, ln] * alive3
        c = conv.astype(bf16)
        c_ref[:, ln] = c
        r = jax.nn.sigmoid(dot(c, wa_ref[k]) + ba_ref[:, ln])
        i = jax.nn.sigmoid(dot(c, wi_ref[k]) + bi_ref[:, ln])
        r_ref[:, ln] = r
        i_ref[:, ln] = i
        decay = r * vec_ref[4:5, ln]
        mult = (1.0 - keep) + keep * jnp.sqrt(one_minus_exp(2.0 * decay))
        carry = jnp.exp(-decay) * keep
        carry_ref[:, ln] = carry
        cbuf[k] = carry
        dbuf[k] = mult * i * c.astype(f32)
    blocks = chan // 128
    hh = [jnp.zeros((SEGS, 128), f32) for _ in range(blocks)]
    pp = [jnp.ones((SEGS, 128), f32) for _ in range(blocks)]
    for j in range(length):
        rows = pl.ds(j, SEGS, stride=length)
        for k in range(blocks):
            a = cbuf[k, rows, :]
            hh[k] = a * hh[k] + dbuf[k, rows, :]
            pp[k] = a * pp[k]
            hs[k, rows, :] = hh[k]
            ps[k, rows, :] = pp[k]
    for k in range(blocks):
        ln = slice(k * 128, (k + 1) * 128)
        prow = run[0:1, ln]
        hrow = run[1:2, ln]
        for s in range(SEGS):
            rows = slice(s * length, (s + 1) * length)
            pseg = ps[k, rows, :]
            h_ref[rows, ln] = hs[k, rows, :] + pseg * hrow
            p_ref[rows, ln] = pseg * prow
            hrow = hh[k][s : s + 1, :] + pp[k][s : s + 1, :] * hrow
            prow = pp[k][s : s + 1, :] * prow
        run[0:1, ln] = prow
        run[1:2, ln] = hrow
        end_ref[0:1, ln] = prow
        end_ref[1:2, ln] = hrow


def recur(chain, mine, xe, wx, bx, g1, wa, wi, conv_w, conv_b, ba, bi, lam, u, flags, tb):
    rows, chan = u.shape
    spec = lambda w: pl.BlockSpec((tb, w), lambda b: (b, 0))
    fixed = [xe, wx, bx, g1, wa, wi, conv_w, conv_b, ba, bi, lam]
    full = lambda shape: (whole(shape), shape, f32)
    return chain(
        recur_kernel, [mine, *fixed, u, flags],
        [SMEM] + [whole(a.shape) for a in fixed] + [spec(chan), spec(1)],
        [pinned(spec(chan), (rows, chan), bf16)]
        + [pinned(spec(chan), (rows, chan), f32)] * 3
        + [(spec(chan), (rows, chan), f32)] * 2
        + [full((2, chan)), full((HALO, chan)), full((HALO, 128)), full((8, chan))],
        "recur", grid=(rows // tb,),
        scratch=[
            pltpu.VMEM((tb + HALO, chan), f32),
            pltpu.VMEM((tb + HALO, 128), f32),
            *[pltpu.VMEM((chan // 128, tb, 128), f32)] * 4,
            pltpu.VMEM((2, chan), f32),
        ],
    )


def entering(ends_ref, mine, backward):
    count = ends_ref.shape[0]
    total = jnp.zeros_like(ends_ref[0, 1:2, :])
    for s in range(count - 1):
        at = count - 1 - s if backward else s
        new = ends_ref[at, 0:1, :] * total + ends_ref[at, 1:2, :]
        inside = at > mine if backward else at < mine
        total = jnp.where(inside, new, total)
    return total


def out_kernel(mine_ref, ends_ref, wo_ref, h_ref, p_ref, ypre_ref, state_ref, gl_ref, part_ref):
    into = entering(ends_ref, mine_ref[0], False)
    state = h_ref[...] + p_ref[...] * into
    state_ref[...] = state
    gl = (gelu(ypre_ref[...]) * state).astype(bf16)
    gl_ref[...] = gl
    part_ref[...] = dot(gl, wo_ref[...]).astype(bf16)


def by_parts(chain, kernel, chunk, fixed, arrived, chunked, name, **more):
    off, tb = chunk
    step = STEP if off % STEP == 0 and tb % STEP == 0 else tb
    rows, width = chunked[0].shape
    inner = pl.BlockSpec((step, width), lambda i: (i, 0))
    first = off // step
    outer = pl.BlockSpec((step, width), lambda i: (first + i, 0))
    return chain(
        kernel, list(fixed) + list(arrived) + [in_hbm(a) for a in chunked],
        [SMEM if a.dtype == jnp.int32 else whole(a.shape) for a in fixed]
        + [inner] * len(arrived) + [outer] * len(chunked),
        [pinned(outer, (rows, width), bf16)], name, grid=(tb // step,), **more,
    )


def chunk_call(chain, kernel, chunk, fixed, chunked, outs, own, name, free=False, held=(), **more):
    off, tb = chunk
    rows = chunked[0].shape[0]
    ins = [SMEM if a.dtype == jnp.int32 else whole(a.shape) for a in fixed]
    ins += [VMEM] * len(held)
    return chain(
        kernel, list(fixed) + [in_vmem(a) for a in held] + [a if free else in_hbm(a) for a in chunked],
        ins + [rows_at(off, tb, a.shape[1]) for a in chunked],
        [pinned(rows_at(off, tb, w), (rows, w), d) for w, d in outs]
        + [(whole(s), s, d) for s, d in own],
        name, **more,
    )


def out_chunk(chain, chunk, mine, h, p, ypre, ends, wo, carried):
    chan, width = wo.shape
    return chunk_call(
        chain, out_kernel, chunk, [mine, ends, wo], [h, p, ypre], [(chan, f32), (chan, bf16)],
        [((chunk[1], width), bf16)], "out_proj", carried=carried, free=True,
    )


def slopes_kernel(
    mine_ref, ends_ref, vec_ref, r_ref, i_ref, carry_ref, c_ref, state_ref, before_ref, flag_ref,
    *rest,
):
    a_ref, b_ref, d_ref, g_ref, sext = rest[-5:]
    tb = r_ref.shape[0]
    b = pl.program_id(0)
    sext[8:, :] = state_ref[...]
    sext[:8, :] = before_ref[...]

    @pl.when(b == 0)
    def _():
        sext[7:8, :] = entering(ends_ref, mine_ref[0], False)

    keep = 1.0 - flag_ref[...].astype(f32)
    sp = vec_ref[4:5, :]
    r = r_ref[...]
    i = i_ref[...]
    c = c_ref[...].astype(f32)
    m2 = one_minus_exp(2.0 * (r * sp))
    m = jnp.sqrt(m2)
    mult = (1.0 - keep) + keep * m
    prior = sext[7 : 7 + tb, :]
    grad = prior * carry_ref[...] - i * c * keep * (1.0 - m2) / m
    gr = grad * r
    g_ref[...] = gr
    a_ref[...] = -gr * sp * (1.0 - r)
    mi = mult * i
    b_ref[...] = mi * c * (1.0 - i)
    d_ref[...] = mi


def slopes(chain, mine, ends, vec, r, i, carry, c, state, flags, tb, ahead):
    rows, chan = r.shape
    spec = lambda w: pl.BlockSpec((tb, w), lambda b: (b, 0))
    before = pl.BlockSpec((8, chan), lambda b: (jnp.maximum(b * (tb // 8) - 1, 0), 0))
    return chain(
        slopes_kernel,
        [mine, ends, vec] + [in_hbm(a) for a in (r, i, carry, c, state, state)] + [flags]
        + [in_vmem(a) for a in ahead],
        [SMEM, whole(ends.shape), whole(vec.shape)] + [spec(chan)] * 5 + [before, spec(1)]
        + [VMEM] * len(ahead),
        [pinned(spec(chan), (rows, chan), f32)] * 4,
        "slopes", grid=(rows // tb,), scratch=[pltpu.VMEM((tb + 8, chan), f32)],
    )


def pick(mid_ref, t_ref, far_ref):
    mid = mid_ref[0] == 1
    return jnp.where(mid, t_ref[...], far_ref[...])


def mlp_kernel(
    mid_ref, g2_ref, t_ref, far_ref, wg_ref, wu_ref, wd_ref, x_ref, cot_ref,
    rec_ref, n2_ref, hid_ref, dg_ref, du_ref, mpart_ref, dpart_ref,
):
    rec = pick(mid_ref, t_ref, far_ref)
    rec_ref[...] = rec
    n2 = norm(x_ref[...].astype(f32) + rec.astype(f32), g2_ref[...])
    n2_ref[...] = n2
    gpre = dot(n2, wg_ref[...])
    up = dot(n2, wu_ref[...])
    dh = dot_nt(cot_ref[...], wd_ref[...])
    act, slope = gelu_both(gpre)
    hid = (act * up).astype(bf16)
    dg = (dh * up * slope).astype(bf16)
    du = (dh * act).astype(bf16)
    hid_ref[...] = hid
    dg_ref[...] = dg
    du_ref[...] = du
    dpart_ref[...] = (dot_nt(dg, wg_ref[...]) + dot_nt(du, wu_ref[...])).astype(bf16)
    mpart_ref[...] = dot(hid, wd_ref[...]).astype(bf16)


def mlp_chunk(chain, chunk, group, mid, t, far, g2, wg, wu, wd, x, cot, carried, mpart):
    rows, width = x.shape
    hidden = wg.shape[1]
    off, tb = chunk
    base, size = group
    put = lambda w, d=bf16: pinned(rows_at(off, tb, w), (rows, w), d)
    return chain(
        mlp_kernel, [mid, g2, t, far, *[in_vmem(a) for a in (wg, wu, wd)], in_hbm(x), in_hbm(cot)],
        [SMEM, whole(g2.shape), whole(t.shape), whole(far.shape), VMEM, VMEM, VMEM]
        + [rows_at(off, tb, width)] * 2,
        [put(width), put(width), put(hidden), put(hidden), put(hidden)]
        + [(rows_at(off - base, tb, width), (size, width), bf16)]
        + [(whole((tb, width)), (tb, width), bf16)],
        "mlp", carried=(carried or [None] * 5) + [mpart], loose=(5,), mib=36,
    )


def back_kernel(
    mid_ref, t_ref, far_ref, g2_ref, wo_ref, run_ref,
    x_ref, rec_ref, cot_ref, state_ref, ypre_ref, carry_ref,
    drec_ref, branch_ref, adj_ref, q_ref, end_ref, dg2_ref, cbuf, dbuf, al, ql,
):
    tb = x_ref.shape[0]
    chan = wo_ref.shape[0]
    length = tb // SEGS
    dn = pick(mid_ref, t_ref, far_ref).astype(f32)
    x2 = x_ref[...].astype(f32) + rec_ref[...].astype(f32)
    inv = lax.rsqrt(jnp.mean(x2 * x2, axis=-1, keepdims=True) + EPS)
    hat = x2 * inv
    dh = dn * hat
    dg2_ref[...] = jnp.sum(dh, axis=0, keepdims=True)
    g2 = g2_ref[...]
    dot_mean = jnp.mean(dh * g2, axis=-1, keepdims=True)
    dx2 = cot_ref[...].astype(f32) + inv * (dn * g2 - hat * dot_mean)
    drec = dx2.astype(bf16)
    drec_ref[...] = drec
    dgl = dot_nt(drec, wo_ref[...])
    y, slope = gelu_both(ypre_ref[...])
    branch_ref[...] = (dgl * state_ref[...] * slope).astype(bf16)
    dstate = dgl * y
    blocks = chan // 128
    for k in range(blocks):
        ln = slice(k * 128, (k + 1) * 128)
        cbuf[k] = carry_ref[:, ln]
        dbuf[k] = dstate[:, ln]
    ee = [jnp.zeros((SEGS, 128), f32) for _ in range(blocks)]
    qq = [jnp.ones((SEGS, 128), f32) for _ in range(blocks)]
    for j in range(length - 1, -1, -1):
        rows = pl.ds(j, SEGS, stride=length)
        for k in range(blocks):
            a = cbuf[k, rows, :]
            adj = dbuf[k, rows, :] + ee[k]
            al[k, rows, :] = adj
            ql[k, rows, :] = qq[k]
            ee[k] = a * adj
            qq[k] = a * qq[k]
    for k in range(blocks):
        ln = slice(k * 128, (k + 1) * 128)
        qrow = run_ref[0:1, ln]
        erow = run_ref[1:2, ln]
        for s in range(SEGS - 1, -1, -1):
            rows = slice(s * length, (s + 1) * length)
            qseg = ql[k, rows, :]
            adj_ref[rows, ln] = al[k, rows, :] + qseg * erow
            q_ref[rows, ln] = qseg * qrow
            qend = qq[k][s : s + 1, :]
            erow = ee[k][s : s + 1, :] + qend * erow
            qrow = qend * qrow
        end_ref[0:1, ln] = qrow
        end_ref[1:2, ln] = erow


def back_chunk(chain, chunk, mid, t, far, g2, wo, run, x, rec, cot, state, ypre, carry, carried):
    chan, width = wo.shape
    return chunk_call(
        chain, back_kernel, chunk, [mid, t, far, g2, wo, run], [x, rec, cot, state, ypre, carry],
        [(width, bf16), (chan, bf16), (chan, f32), (chan, f32)],
        [((2, chan), f32), ((1, width), f32)], "mid_back", carried=carried,
        scratch=[pltpu.VMEM((chan // 128, chunk[1], 128), f32)] * 4,
    )


def gates_kernel(
    mine_ref, ends_ref, vec_ref, wa_ref, wi_ref, ue_ref, ke_ref,
    adj_ref, q_ref, a_ref, b_ref, d_ref, g_ref, c_ref, u_ref, before_ref, flag_ref, flag_before_ref,
    branch_ref, du_ref, tail_ref, edge_ref, gwa_ref, gwi_ref, sums_ref, uext, kext, e1, e2, e3,
):
    tb, chan = adj_ref.shape
    step = pl.program_id(0)
    steps = pl.num_programs(0)
    side = wa_ref.shape[1]
    vec = lambda k: vec_ref[k : k + 1, :]

    @pl.when(step == 0)
    def _():
        for e in (e1, e2, e3):
            e[tb:, :] = jnp.zeros((8, chan), f32)
        gwa_ref[...] = jnp.zeros_like(gwa_ref)
        gwi_ref[...] = jnp.zeros_like(gwi_ref)
        sums_ref[...] = jnp.zeros_like(sums_ref)

    @pl.when(step > 0)
    def _():
        for e in (e1, e2, e3):
            e[tb:, :] = e[:8, :]

    uext[HALO:, :] = u_ref[...].astype(f32)
    kext[HALO:, :] = jnp.broadcast_to(1.0 - flag_ref[...].astype(f32), (tb, 128))

    @pl.when(step == steps - 1)
    def _():
        uext[:HALO, :] = ue_ref[...]
        kext[:HALO, :] = ke_ref[...]

    @pl.when(step < steps - 1)
    def _():
        uext[:HALO, :] = before_ref[...].astype(f32)
        kext[:HALO, :] = jnp.broadcast_to(1.0 - flag_before_ref[...].astype(f32), (HALO, 128))

    into = entering(ends_ref, mine_ref[0], True)
    keep, alive2, alive3 = spread_masks(flag_ref, kext, None)

    def add(k, ln, value):
        sums_ref[k : k + 1, ln] += jnp.sum(value, axis=0, keepdims=True)

    for k in range(chan // side):
        ln = slice(k * side, (k + 1) * side)
        adj = adj_ref[:, ln] + q_ref[:, ln] * into[:, ln]
        add(2, ln, adj * g_ref[:, ln])
        da = (adj * a_ref[:, ln]).astype(bf16)
        di = (adj * b_ref[:, ln]).astype(bf16)
        add(0, ln, da.astype(f32))
        add(1, ln, di.astype(f32))
        gwa_ref[k] += dot_tn(c_ref[:, ln], da)
        gwi_ref[k] += dot_tn(c_ref[:, ln], di)
        dconv = adj * d_ref[:, ln] + dot_nt(da, wa_ref[k]) + dot_nt(di, wi_ref[k])
        add(3, ln, dconv)
        add(4, ln, dconv * uext[HALO:, ln])
        mk = dconv * keep
        e1[:tb, ln] = mk
        add(5, ln, mk * uext[HALO - 1 : HALO - 1 + tb, ln])
        mk = dconv * alive2
        e2[:tb, ln] = mk
        add(6, ln, mk * uext[HALO - 2 : HALO - 2 + tb, ln])
        mk = dconv * alive3
        e3[:tb, ln] = mk
        add(7, ln, mk * uext[HALO - 3 : HALO - 3 + tb, ln])
        v = lambda j: vec_ref[j : j + 1, ln]
        du = v(0) * dconv + v(1) * e1[1 : 1 + tb, ln]
        du = du + v(2) * e2[2 : 2 + tb, ln] + v(3) * e3[3 : 3 + tb, ln]
        low = du.astype(bf16)
        du_ref[:, ln] = low
        add(8, ln, low.astype(f32))
        add(9, ln, branch_ref[:, ln].astype(f32))

        @pl.when(step == 0)
        def _():
            tail_ref[:, ln] = du[tb - HALO :, :]
            sums_ref[8:9, ln] -= jnp.sum(low[tb - HALO :, :].astype(f32), axis=0, keepdims=True)

    @pl.when(step == steps - 1)
    def _():
        edge_ref[...] = jnp.zeros_like(edge_ref)
        edge_ref[5:6, :] = vec(3) * e3[0:1, :]
        edge_ref[6:7, :] = vec(2) * e2[0:1, :] + vec(3) * e3[1:2, :]
        edge_ref[7:8, :] = vec(1) * e1[0:1, :] + vec(2) * e2[1:2, :] + vec(3) * e3[2:3, :]
        sums_ref[2:3, :] = sums_ref[2:3, :] * vec(5)


def gates_back(chain, mine, ends, vec, wa, wi, ue, ke, adj, q, slope4, c, u, flags, branch, tb):
    rows, chan = adj.shape
    n = rows // tb
    spec = lambda w: pl.BlockSpec((tb, w), lambda b: (n - 1 - b, 0))
    per = tb // HALO
    before = lambda w: pl.BlockSpec((HALO, w), lambda b: (jnp.maximum((n - 1 - b) * per - 1, 0), 0))
    full = lambda shape: (whole(shape), shape, f32)
    fixed = [ends, vec, wa, wi, ue, ke]
    return chain(
        gates_kernel,
        [mine, *fixed] + [in_hbm(a) for a in (adj, q, *slope4, c, u, u)] + [flags, flags]
        + [in_hbm(branch)],
        [SMEM] + [whole(a.shape) for a in fixed] + [spec(chan)] * 8
        + [before(chan), spec(1), before(1), spec(chan)],
        [
            pinned(spec(chan), (rows, chan), bf16), full((HALO, chan)), full((8, chan)), full(wa.shape),
            full(wi.shape), full((16, chan)),
        ],
        "gates_back", grid=(n,), mib=40, cost=LONG_G,
        scratch=[pltpu.VMEM((tb + HALO, chan), f32), pltpu.VMEM((tb + HALO, 128), f32)]
        + [pltpu.VMEM((tb + 8, chan), f32)] * 3,
    )


def in_kernel(wy_ref, wx_ref, x_ref, branch_ref, du_ref, part_ref, dg1_ref):
    part = dot_nt(branch_ref[...], wy_ref[...]) + dot_nt(du_ref[...], wx_ref[...])
    part_ref[...] = part.astype(bf16)
    x = x_ref[...].astype(f32)
    inv = lax.rsqrt(jnp.mean(x * x, axis=-1, keepdims=True) + EPS)
    dg1_ref[...] = jnp.sum(part * (x * inv), axis=0, keepdims=True)


def in_chunk(chain, chunk, wy, wx, x, branch, du):
    width = x.shape[1]
    return chunk_call(
        chain, in_kernel, chunk, [wy, wx], [x, branch, du], [],
        [((chunk[1], width), bf16), ((1, width), f32)], "in_back",
    )


def result_kernel(mid_ref, t_ref, far_ref, x_ref, rec_ref, out_ref):
    total = x_ref[...].astype(f32) + rec_ref[...].astype(f32)
    out_ref[...] = (total + pick(mid_ref, t_ref, far_ref).astype(f32)).astype(bf16)


def result_chunk(chain, chunk, mid, t, far, x, rec, carried):
    return by_parts(
        chain, result_kernel, chunk, [mid], [t, far], [x, rec], "result", carried=carried
    )


def last_kernel(mid_ref, g1_ref, t_ref, far_ref, x_ref, dx2_ref, out_ref):
    dn = pick(mid_ref, t_ref, far_ref).astype(f32) * g1_ref[...]
    x = x_ref[...].astype(f32)
    inv = lax.rsqrt(jnp.mean(x * x, axis=-1, keepdims=True) + EPS)
    hat = x * inv
    mean = jnp.mean(dn * hat, axis=-1, keepdims=True)
    out_ref[...] = (dx2_ref[...].astype(f32) + inv * (dn - hat * mean)).astype(bf16)


def last_chunk(chain, chunk, mid, t, far, g1, x, dx2, carried, cost):
    return by_parts(
        chain, last_kernel, chunk, [mid, g1], [t, far], [x, dx2], "stream_grad", carried=carried,
        cost=cost,
    )


def weight_grad(chain, a, b, at, columns, db, carried):
    height, wide = a.shape[1], b.shape[1]

    def kernel(a_ref, b_ref, out_ref):
        out_ref[...] = dot_tn(a_ref[...], b_ref[...]).astype(bf16)

    rows = a.shape[0]
    return chain(
        kernel, [in_hbm(a), in_hbm(b)],
        [pl.BlockSpec((rows, db), lambda i: (0, i)), whole(b.shape)],
        [pinned(pl.BlockSpec((db, wide), lambda i: (i, at)), (height, columns), bf16)],
        "weight_grad", grid=(height // db,), carried=carried, mib=24,
    )


def widen(chain, total, name):
    rows, columns = total.shape
    third = columns // 3

    def kernel(t_ref, a_ref, b_ref, c_ref):
        a_ref[...] = t_ref[:, :third].astype(f32)
        b_ref[...] = t_ref[:, third : 2 * third].astype(f32)
        c_ref[...] = t_ref[:, 2 * third :].astype(f32).T

    shapes = [(rows, third), (rows, third), (third, rows)]
    return chain(
        kernel, [total], [whole(total.shape)], [(whole(s), s, f32) for s in shapes], name
    )


def add_pair(chain, a, b):
    def kernel(a_ref, b_ref, out_ref):
        out_ref[...] = (a_ref[...].astype(f32) + b_ref[...].astype(f32)).astype(out_ref.dtype)

    return chain(
        kernel, [a, b], [whole(a.shape), whole(b.shape)], [(whole(a.shape), a.shape, a.dtype)],
        "hop_sum",
    )[0]


class Fold:
    def __init__(self, chain, axis):
        self.chain = chain
        self.axis = axis
        self.line = lax.axis_size(axis) == 4

    def start(self, part):
        self.part = part
        if self.line:
            self.got = lax.ppermute(part, self.axis, [(0, 1), (3, 2)])
        else:
            self.t = self.far = lax.psum(part, self.axis)

    def swap(self):
        if self.line:
            self.part = add_pair(self.chain, self.part, self.got)
            self.got = lax.ppermute(self.part, self.axis, [(1, 2), (2, 1)])

    def back(self):
        if self.line:
            self.t = add_pair(self.chain, self.part, self.got)
            self.far = lax.ppermute(self.t, self.axis, [(1, 0), (2, 3)])

    def pair(self):
        return self.t, self.far


class Exchange:
    def __init__(self, chain, value, axis):
        self.chain, self.axis, self.value = chain, axis, value
        self.n = lax.axis_size(axis)
        self.bit = 1
        if self.n & (self.n - 1):
            self.value = lax.psum(value, axis)
            self.bit = self.n
        self.send()

    def send(self):
        if self.bit < self.n:
            route = [(i, i ^ self.bit) for i in range(self.n)]
            self.got = lax.ppermute(self.value, self.axis, route)

    def step(self):
        if self.bit < self.n:
            self.value = add_pair(self.chain, self.value, self.got)
            self.bit *= 2
            self.send()

    def finish(self):
        while self.bit < self.n:
            self.step()
        return self.value


def split(sizes):
    chunks, off = [], 0
    for size in sizes:
        chunks.append((off, size))
        off += size
    return chunks


def body(
    x, prescale, wy, by, wx, bx, conv_w, conv_b, wa, ba, wi, bi, lam, wo, midscale, wg, wu, wd,
    resets, cot,
):
    rows, width = x.shape
    chan = wy.shape[1]
    hidden = wg.shape[1]
    blocks, side = wa.shape[:2]
    n_seq = lax.axis_size("seq")
    n_head = lax.axis_size("head")
    mine = lax.axis_index("seq").astype(jnp.int32)[None]
    me = lax.axis_index("head")
    mid = ((me == 1) | (me == 2)).astype(jnp.int32)[None]
    chain = Chain()
    tb = 256
    sizes = FIRST if sum(FIRST) == rows else [rows // 4] * 4
    one = split(sizes)[::-1]
    sizes = LAST if sum(LAST) == rows else [rows // 4] * 4
    two = split(sizes)

    g1, g2 = prescale[None], midscale[None]
    flags = resets[:, None]
    packed = jnp.concatenate(
        [x[rows - HALO :], jnp.broadcast_to(flags[rows - HALO :], (HALO, 128)).astype(bf16)], axis=1
    )
    forward = [(i, i + 1) for i in range(n_seq - 1)]
    backward = [(i + 1, i) for i in range(n_seq - 1)]
    xe = lax.ppermute(packed, "seq", forward)
    n1, ypre, u = project(chain, x, wy, wx, by[None], bx[None], g1, tb)
    c, carry, r, i, h, p, end, ue, ke, vec = recur(
        chain, mine, xe, wx, bx[None], g1, wa, wi, conv_w, conv_b[None], ba[None], bi[None],
        lam[None], u, flags, tb,
    )
    ends = lax.all_gather(end, "seq")

    n = len(one)
    rec_f = [Fold(chain, "head") for _ in one]
    n2_f = [Fold(chain, "head") for _ in one]
    n1_f = [Fold(chain, "head") for _ in two]
    groups = one
    mlp_f = [Fold(chain, "head") for _ in groups]
    d = {}

    kept = None
    for k in range(n):
        *kept, part = out_chunk(chain, one[k], mine, h, p, ypre, ends, wo, kept)
        rec_f[k].start(part)
    state, gl = kept
    slope4 = slopes(
        chain, mine, ends, vec, r, i, carry, c, state, flags, tb, (wg, wu, wd)
    )

    def mlp(k):
        g = k * len(groups) // n
        *d["mlp"], d["mp", g], dp = mlp_chunk(
            chain, one[k], groups[g], mid, *rec_f[k].pair(), g2, wg, wu, wd, x, cot, d.get("mlp"),
            d.get(("mp", g)),
        )
        n2_f[k].start(dp)

    def back(k):
        run = d.get("run")
        if run is None:
            run = jnp.concatenate([jnp.ones((1, chan), f32), jnp.zeros((1, chan), f32)])
        *d["back"], d["run"], dg2 = back_chunk(
            chain, one[k], mid, *n2_f[k].pair(), g2, wo, run, x, d["mlp"][0], cot, state, ypre,
            carry, d.get("back"),
        )
        d["g2"] = d.get("g2", 0.0) + dg2

    def big(k):
        rec, n2, hid, dg, du2 = d["mlp"]
        a, b = ((n2, dg), (n2, du2), (cot, hid))[k]
        d["big"] = weight_grad(chain, a, b, k, 3 * hidden, 512, d.get("big"))

    def start_mlp(k):
        mlp_f[k].start(d["mp", k])

    def result(k):
        d["result"] = result_chunk(
            chain, groups[k], mid, *mlp_f[k].pair(), x, d["mlp"][0], d.get("result")
        )

    def scatter():
        d["big_sum"] = lax.psum_scatter(d["big"][0], "seq", scatter_dimension=0, tiled=True)

    def gather():
        d["ends"] = lax.all_gather(d["run"], "seq")

    def gates():
        drec, branch, adj, q = d["back"]
        d["du"], d["tail"], edge, d["gwa"], d["gwi"], d["sums"] = gates_back(
            chain, mine, d["ends"], vec, wa, wi, ue, ke, adj, q, slope4, c, u, flags, branch, tb
        )
        d["edge"] = lax.ppermute(edge, "seq", backward)

    def patched():
        patch = d["tail"] + jnp.concatenate([jnp.zeros((HALO - 8, chan), f32), d["edge"]])
        patch = patch.astype(bf16)
        d["du"] = lax.dynamic_update_slice(d["du"], patch, (rows - HALO, 0))
        d["sums"] = d["sums"].at[8].add(jnp.sum(patch.astype(f32), axis=0))

    def inner(k):
        part, dg1 = in_chunk(chain, two[k], wy, wx, x, d["back"][1], d["du"])
        d["g1"] = d.get("g1", 0.0) + dg1
        n1_f[k].start(part)

    def lru_weights(k):
        drec, branch, adj, q = d["back"]
        a, b = ((n1, branch), (n1, d["du"]), (drec, gl))[k]
        d["small"] = weight_grad(chain, a, b, k, 3 * chan, 768, d.get("small"))

    def scatter_small():
        d["small_sum"] = lax.psum_scatter(d["small"][0], "seq", scatter_dimension=0, tiled=True)

    def stacked():
        gains = jnp.concatenate([d["g1"], d["g2"] * (1.0 / n_head)])
        pieces = [d[name].reshape(-1, side) for name in ("gwa", "gwi", "sums")]
        pieces.append(gains.reshape(-1, side))
        cuts = [0]
        for piece in pieces:
            cuts.append(cuts[-1] + piece.shape[0])
        d["cuts"] = cuts
        stack = jnp.concatenate(pieces + [jnp.zeros((-cuts[-1] % 16, side), f32)]).astype(bf16)
        d["stack"] = Exchange(chain, stack, "seq")

    def stack_step():
        d["stack"].step()

    def head_start():
        d["total"] = d["stack"].finish()
        d["gains"] = Exchange(chain, d["total"][d["cuts"][3] :], "head")

    def head_step():
        d["gains"].step()

    def widen_big():
        d["big_out"] = widen(chain, d["big_sum"], "mlp_grads")

    def widen_small():
        d["small_out"] = widen(chain, d["small_sum"], "lru_grads")

    def last(k):
        d["last"] = last_chunk(
            chain, two[k], mid, *n1_f[k].pair(), g1, x, d["back"][0], d.get("last"),
            LONG if k == len(two) - 1 else None,
        )

    calls = {
        "Rs": lambda k: rec_f[k].swap(), "Rb": lambda k: rec_f[k].back(), "M": mlp,
        "Ns": lambda k: n2_f[k].swap(), "Nb": lambda k: n2_f[k].back(), "B": back, "W": big,
        "I": inner, "X": patched, "V": lru_weights, "As": lambda k: n1_f[k].swap(),
        "Ab": lambda k: n1_f[k].back(), "L": last, "P": start_mlp, "T": result,
        "Ps": lambda k: mlp_f[k].swap(), "Pb": lambda k: mlp_f[k].back(), "scatter": scatter,
        "gather": gather, "gates": gates, "scatter_small": scatter_small, "stack": stacked,
        "stack_step": stack_step, "head": head_start, "head_step": head_step, "big": widen_big,
        "small": widen_small,
    }
    for line in ORDER:
        for step in line.split():
            name = step.rstrip("0123456789")
            calls[name](*([int(step[len(name) :])] if step != name else []))

    g_y, g_x, g_o = d["small_out"]
    g_gate, g_up, g_down = d["big_out"]
    cuts = d["cuts"]
    total = d["total"].astype(f32)
    gains = d["gains"].finish()[: cuts[4] - cuts[3]].astype(f32).reshape(2, width)
    gwa = total[: cuts[1]].reshape(wa.shape)
    gwi = total[cuts[1] : cuts[2]].reshape(wi.shape)
    sums = total[cuts[2] : cuts[3]].reshape(16, chan)
    piece = width // n_seq
    gains = lax.dynamic_slice(gains, (0, mine[0] * piece), (2, piece))
    return (
        d["result"][0], d["last"][0], gains[0], g_y, sums[9], g_x, sums[8], sums[4:8], sums[3],
        gwa, sums[0], gwi, sums[1], sums[2], g_o, gains[1], g_gate, g_up, g_down,
    )


LONG = 3 * 10**10
LONG_G = 10**13
STEP = 128
FIRST = [256, 256, 256, 256]
LAST = [256, 256, 256, 256]

ORDER = [
    "Rs0 Rs1 Rb0 Rs2", "Rb1 M0 P0 Rs3", "Rb2 M1 P1 Ns0", "Rb3 M2 P2 Ns1", "Nb0 M3 P3 Ns2",
    "Nb1 W0 B0 W1", "Ns3 Ps0 Nb2 W2", "scatter B1 Nb3 Ps1", "Pb0 B2 Ps2 Pb1",
    "B3 gather gates Ps3", "Pb2 T0 I0 I1", "I2 T1 X I3", "Pb3 T2 V0 As0",
    "V2 V1 scatter_small stack", "As1 Ab0 T3 stack_step", "As2 Ab1 L0 stack_step",
    "As3 Ab2 L1 stack_step", "head Ab3 L2 head_step", "head_step L3 big small",
]


def solution(mesh):
    col, row, both = P(None, "head"), P("head", None), P("seq", "head")
    head, seq, cube = P("head"), P("seq"), P("head", None, None)
    tokens = P("seq", None)
    in_specs = (
        tokens, P(), col, head, col, head, col, head, cube, head, cube, head, head, row, P(), col,
        col, row, seq, tokens,
    )
    out_specs = (
        tokens, tokens, seq, both, head, both, head, col, head, cube, head, cube, head, head,
        P("head", "seq"), seq, both, both, P("head", "seq"),
    )
    return jax.shard_map(body, mesh=mesh, in_specs=in_specs, out_specs=out_specs, check_vma=False)
```
